256 devices in a mesh: dp: 16 (over x, y), tensor: 16 (over z, core).
Axes of the slice: x: 4, y: 4, z: 8, core: 2. Of those that a mesh axis runs over, the one named last changes fastest.
Arguments:
- activations: bfloat16 [32, 1024, 4096], P('dp', 'tensor'), may hold values from -6 to 6
- out_grads: bfloat16 [32, 1024, 8192], P('dp', None, 'tensor')
- lengths: int32 [32], P('dp'), may hold values from 128 to 1024, as said below
- clip_bound: float32 [1], replicated, may hold values from 2867.2 to 6389.76
- noise: float32 [4096, 8192], P('dp', 'tensor'), may hold values from -4 to 4
Outputs:
- private_grad: float32 [4096, 8192], P('dp', 'tensor')
The draws below stay inside these ranges and needn't reach their ends.
Inputs may be any that keep to these rules, and one draw needn't show every extreme that they name: `lengths`: at least one example uses all 1024 positions.
All inputs are finite; a program needn't handle non-finite values.
Results may differ from the reference program's by a relative error of at most 0.0003.
Values may be sent and summed in bfloat16 or wider, within the bound.
No kernel may reach another device: no remote copies, remote signals or barrier semaphores. Data moves between devices by JAX's collectives and lax.ppermute only.
A program may use at most 128 MiB of HBM per device.

```python
import math
import jax
import jax.numpy as jnp
from jax import lax

D = 8192
DI = 4096
S = 1024
EXAMPLES = 32


def draw_out_grads(key, part):
    key = jax.random.fold_in(key, 11)
    key_vals, key_cols = jax.random.split(key, 2)
    column_pos = jnp.arange(D, dtype=jnp.float32) / D
    ramp = jnp.exp(jnp.log(3.0) * (column_pos - 0.5))
    spread = jnp.exp(jax.random.uniform(key_cols, (D,), jnp.float32, jnp.log(0.5), jnp.log(2.0)))
    values = jax.random.normal(key_vals, (EXAMPLES, S, D), jnp.float32)
    values = values * (ramp * spread)[None, None, :] / jnp.sqrt(jnp.float32(S))
    return values.astype(jnp.bfloat16)


def draw_lengths(key, part):
    key = jax.random.fold_in(key, 23)
    key_len, key_full = jax.random.split(key)
    drawn = jax.random.randint(key_len, (EXAMPLES,), S // 8, S + 1, jnp.int32)
    chosen = jax.random.randint(key_full, (), 0, EXAMPLES, jnp.int32)
    return drawn.at[chosen].set(S)


def levels(stream_key, dims, shards, low, top_value):
    def one(axis_at, shards_of):
        heights = jax.random.uniform(jax.random.fold_in(jax.random.fold_in(stream_key, 6), axis_at), (shards_of,), jnp.float32, low / len(shards), top_value / len(shards))
        return jnp.repeat(jnp.exp(heights), dims[axis_at] // shards_of).reshape((-1,) + (1,) * (len(dims) - axis_at - 1))

    loudness = one(*shards[0])
    for cut in shards[1:]:
        loudness = loudness * one(*cut)
    return loudness


def scatter_about(rng, extent, deviation, most, cuts=(), kind=jnp.bfloat16):
    level = levels(rng, extent, cuts, -0.22, 0.18) if cuts else 1.0
    values = jax.random.normal(rng, extent, jnp.float32) * deviation * level
    return jnp.minimum(jnp.maximum(values, -most), most).astype(kind)


def setup_inputs(seed: int = 0) -> dict:
    keys = jax.random.split(jax.random.key(seed), 6)
    activations = scatter_about(keys[0], (EXAMPLES, S, DI), 1.0, 6.0, ((0, 16), (1, 16)))
    out_grads = draw_out_grads(jax.random.fold_in(keys[5], 71), 0)
    lengths = draw_lengths(jax.random.fold_in(keys[5], 71), 0)
    clip_bound = jnp.clip(jnp.exp(jax.random.uniform(keys[3], (1,), jnp.float32, math.log(2867.2), math.log(6389.76))), 2867.2, 6389.76)
    noise = scatter_about(keys[4], (DI, D), 0.3, 4.0, ((0, 16), (1, 16)), jnp.float32)
    return dict(activations=activations, out_grads=out_grads, lengths=lengths, clip_bound=clip_bound, noise=noise)


def reference(activations, out_grads, lengths, clip_bound, noise):
    clip_value = clip_bound[0]
    positions = jnp.arange(S, dtype=jnp.int32)[None, :, None]
    masked = jnp.where(positions < lengths[:, None, None], out_grads, jnp.zeros_like(out_grads))

    def add_example(total, inputs):
        acts_one, grads_one = inputs
        product = jnp.dot(acts_one.T, grads_one, preferred_element_type=jnp.float32)
        squares = jnp.sum(product * product)
        factor = clip_value / jnp.maximum(jnp.sqrt(squares), clip_value)
        return (total + factor * product, None)
    summed, unused = lax.scan(add_example, jnp.zeros((DI, D), jnp.float32), (activations, masked))
    return summed / jnp.sqrt(jnp.float32(EXAMPLES)) + noise
```

```python
import functools

import jax
import jax.numpy as jnp
from jax import lax
from jax.experimental import pallas as pl
from jax.experimental.pallas import tpu as pltpu
from jax.sharding import PartitionSpec as P

LANES = 128
EXTRA = 16
TOGETHER = 4
LEAST = 1e-33
PARAMS = pltpu.CompilerParams(vmem_limit_bytes=56 * 1024 * 1024)
RAW = ((0, 64), (64, 32))
CLIPPED = ((128, 128), (96, 32))
OWNED = sum(width for _, width in RAW + CLIPPED)
ARRIVALS = (0, -1, 1, -2, 2, -3, 3, 4)
SMALL = pl.CostEstimate(flops=1, bytes_accessed=1, transcendentals=0)


def part_kernel(parts, acts_ref, part_ref):
    at = 0
    for first, width in parts:
        for tile in range(acts_ref.shape[1] // OWNED * width // LANES):
            owners = range(tile * LANES // width, (tile + 1) * LANES // width)
            pieces = [acts_ref[:, o * OWNED + first : o * OWNED + first + width] for o in owners]
            part_ref[:, at : at + LANES] = jnp.concatenate(pieces, axis=1) if len(pieces) > 1 else pieces[0]
            at += LANES


def part_features(acts, parts):
    examples, shard, features = acts.shape
    taken = features // OWNED * sum(width for _, width in parts)
    return pl.pallas_call(
        functools.partial(part_kernel, parts),
        out_shape=jax.ShapeDtypeStruct((examples * shard, taken), acts.dtype),
        compiler_params=PARAMS,
    )(acts.reshape(examples * shard, features)).reshape(examples, shard, taken)


def coded(values):
    top = jnp.maximum(jnp.max(jnp.abs(values), axis=0, keepdims=True), LEAST)
    exponent = jnp.ceil(jnp.log2(top) - 14.99)
    return jnp.round(values * jnp.exp2(-exponent)), exponent


def narrow(units):
    return units.astype(jnp.int32).astype(jnp.int16)


def packed(tile, owners):
    if owners == 1:
        return [tile]
    width, rows = LANES // owners, tile.shape[0] // owners
    lane = lax.broadcasted_iota(jnp.int32, (rows, LANES), 1)
    out = []
    for owner in range(owners):
        total = None
        for group in range(owners):
            piece = tile[group * rows : (group + 1) * rows]
            shift = (group - owner) * width % LANES
            piece = pltpu.roll(piece, shift, 1) if shift else piece
            total = piece if total is None else jnp.where(lane >= group * width, piece, total)
        out.append(total)
    return out


def packed_row(row, owners):
    return [t[0:1] for t in packed(jnp.broadcast_to(row, (8 * owners, LANES)), owners)]


def lane_sums(product):
    rows = jnp.sum(product * product, axis=0, keepdims=True)
    return sum(rows[:, at : at + LANES] for at in range(0, rows.shape[1], LANES))


def raw_kernel(order_ref, *refs):
    pieces, (grads_ref, coded_ref, exponent_ref, squares_ref, acts, grads, sems) = refs[:-7], refs[-7:]
    example = pl.program_id(0)
    depth = pieces[0].shape[1]

    def copies(e):
        far = pieces[-4 + 2 * e : len(pieces) - 2 + 2 * e]
        sources = [p.at[e] for p in pieces[:-4]] + [p.at[0] for p in far]
        made = [pltpu.make_async_copy(grads_ref.at[e], grads.at[e], sems.at[e, len(sources)])]
        for k, source in enumerate(sources):
            place = pl.ds(pl.multiple_of(order_ref[k] * depth, depth), depth)
            made.append(pltpu.make_async_copy(source, acts.at[e, place], sems.at[e, k]))
        return made

    @pl.when(example == 0)
    def _():
        for copy in copies(0) + copies(1):
            copy.start()
        for copy in copies(0):
            copy.wait()

    @pl.when(example == 1)
    def _():
        for copy in copies(1):
            copy.wait()

    product = jnp.dot(grads[example], acts[example], preferred_element_type=jnp.float32)
    squares_ref[0] = lane_sums(product)
    at = row = 0
    for h, (_, width) in enumerate(RAW):
        together = LANES // width
        rows = product.shape[0] // together
        for tile in range(coded_ref.shape[0] // together):
            units, exponent = coded(product[:, at : at + LANES])
            exponents = packed_row(exponent, together)
            for k, block in enumerate(packed(units, together)):
                coded_ref[tile * together + k, 0, row : row + rows] = narrow(block)
                exponent_ref[tile * together + k, 0, h : h + 1] = exponents[k]
            at += LANES
        row += rows


def raw_products(order, pieces, grads):
    examples, shard, features = pieces[0].shape
    _, columns, positions = grads.shape
    owners = features // sum(width for _, width in RAW)
    rows = columns * features // owners // LANES
    return pl.pallas_call(
        raw_kernel,
        grid=(examples,),
        in_specs=[pl.BlockSpec(memory_space=pltpu.SMEM)]
        + [pl.BlockSpec(memory_space=pltpu.HBM)] * (len(pieces) + 1),
        out_specs=[
            pl.BlockSpec((owners, 1, rows, LANES), lambda e: (0, e, 0, 0)),
            pl.BlockSpec((owners, 1, 8, LANES), lambda e: (0, e, 0, 0)),
            pl.BlockSpec((1, 1, LANES), lambda e: (e, 0, 0)),
        ],
        out_shape=[
            jax.ShapeDtypeStruct((owners, examples, rows, LANES), jnp.int16),
            jax.ShapeDtypeStruct((owners, examples, 8, LANES), jnp.float32),
            jax.ShapeDtypeStruct((examples, 1, LANES), jnp.float32),
        ],
        scratch_shapes=[
            pltpu.VMEM((examples, positions, features), pieces[0].dtype),
            pltpu.VMEM(grads.shape, grads.dtype),
            pltpu.SemaphoreType.DMA((examples, len(order) + 1)),
        ],
        compiler_params=PARAMS,
    )(order, *pieces, grads)


def plain_kernel(acts_ref, grads_ref, squares_ref, product_ref, share_ref):
    devices, _, shard, width = acts_ref.shape
    acts = acts_ref[...].reshape(devices * shard, width)
    product = jnp.dot(grads_ref[0], acts, preferred_element_type=jnp.float32)
    product_ref[0] = product

    @pl.when(pl.program_id(1) == 0)
    def _():
        share_ref[...] = squares_ref[...]

    share_ref[0] += lane_sums(product)


def plain_products(acts, grads, squares):
    devices, examples, shard, features = acts.shape
    _, columns, positions = grads.shape
    width = features // 2
    row = pl.BlockSpec((1, 1, LANES), lambda e, i: (e, 0, 0))
    return pl.pallas_call(
        plain_kernel,
        grid=(examples, features // width),
        in_specs=[
            pl.BlockSpec((devices, 1, shard, width), lambda e, i: (0, e, 0, i)),
            pl.BlockSpec((1, columns, positions), lambda e, i: (e, 0, 0)),
            row,
        ],
        out_specs=[pl.BlockSpec((1, columns, width), lambda e, i: (e, 0, i)), row],
        out_shape=[
            jax.ShapeDtypeStruct((examples, columns, features), jnp.float32),
            jax.ShapeDtypeStruct((examples, 1, LANES), jnp.float32),
        ],
        cost_estimate=SMALL,
        compiler_params=PARAMS,
    )(acts, grads, squares)


def clipped_kernel(clip_ref, shares_ref, wide_ref, thin_ref, exponent_ref, coded_ref):
    examples, columns, _ = wide_ref.shape
    owners = coded_ref.shape[0]
    clip = clip_ref[0]
    blank = jnp.zeros((1, LANES), jnp.float32)
    wide, thin, extra = 0.0, 0.0, [[] for _ in range(owners)]
    for e in range(examples):
        square = jnp.sum(shares_ref[e], axis=1, keepdims=True)
        factor = clip / jnp.maximum(jnp.sqrt(square), clip)
        wide = wide + factor * wide_ref[e]
        thin = thin + factor * thin_ref[e]
        power = jnp.floor(jnp.log2(jnp.maximum(factor, LEAST))) + 1.0
        scaled = factor * jnp.exp2(-power) * 16384.0
        high = jnp.floor(scaled)
        low = jnp.round((scaled - high) * 16384.0)
        for k in range(owners):
            extra[k] += [blank + high, blank + low]
            extra[k] += [exponent_ref[k, e, h : h + 1] + power for h in range(len(RAW))]
    thin_units, exponent = coded(thin)
    thin_units, thin_exponents = packed(thin_units, owners), packed_row(exponent, owners)
    for k in range(owners):
        units, exponent = coded(wide[:, k * LANES : (k + 1) * LANES])
        rows = extra[k] + [exponent, thin_exponents[k]]
        rows = jnp.concatenate(rows + [blank] * (EXTRA - len(rows)), axis=0)
        coded_ref[k, :columns] = narrow(units)
        coded_ref[k, columns : coded_ref.shape[1] - EXTRA] = narrow(thin_units[k])
        coded_ref[k, coded_ref.shape[1] - EXTRA :] = narrow(rows)


def clipped_sums(clip_bound, shares, products, exponents):
    examples, columns, features = products.shape
    owners = exponents.shape[0]
    together = LANES // CLIPPED[1][1]
    rows = columns * features // owners // LANES + EXTRA
    return pl.pallas_call(
        clipped_kernel,
        grid=(owners // together,),
        in_specs=[
            pl.BlockSpec(memory_space=pltpu.SMEM),
            pl.BlockSpec(shares.shape, lambda i: (0, 0, 0)),
            pl.BlockSpec((examples, columns, together * LANES), lambda i: (0, 0, i)),
            pl.BlockSpec((examples, columns, LANES), lambda i: (0, 0, owners + i)),
            pl.BlockSpec((together, examples, 8, LANES), lambda i: (i, 0, 0, 0)),
        ],
        out_specs=pl.BlockSpec((together, rows, LANES), lambda i: (i, 0, 0)),
        out_shape=jax.ShapeDtypeStruct((owners, rows, LANES), jnp.int16),
        cost_estimate=SMALL,
        compiler_params=PARAMS,
    )(clip_bound, shares, products, products, exponents)


def finish_kernel(scale, raw_ref, clipped_ref, noise_ref, out_ref, raw_sum, clipped_sum):
    _, examples, _, _ = raw_ref.shape
    columns = out_ref.shape[1]
    group = pl.program_id(0)

    @pl.when(group == 0)
    def _():
        raw_sum[...] = jnp.zeros_like(raw_sum)
        clipped_sum[...] = jnp.zeros_like(clipped_sum)

    kinds = len(RAW)
    bottom = clipped_sum.shape[0]
    extra = [clipped_ref[g, bottom:].astype(jnp.float32) for g in range(TOGETHER)]
    at = 0
    for h, (_, width) in enumerate(RAW):
        rows = columns * width // LANES
        total = raw_sum[at : at + rows]
        for g in range(TOGETHER):
            row = lambda k: extra[g][k : k + 1]
            for e in range(examples):
                base = e * (2 + kinds)
                weight = (row(base) + row(base + 1) * (1.0 / 16384.0)) * (1.0 / 16384.0) * jnp.exp2(row(base + 2 + h))
                total = total + weight * raw_ref[g, e, at : at + rows].astype(jnp.float32)
        raw_sum[at : at + rows] = total
        at += rows
    at = 0
    for h, (_, width) in enumerate(CLIPPED):
        rows = columns * width // LANES
        total = clipped_sum[at : at + rows]
        for g in range(TOGETHER):
            k = examples * (2 + kinds) + h
            total = total + jnp.exp2(extra[g][k : k + 1]) * clipped_ref[g, at : at + rows].astype(jnp.float32)
        clipped_sum[at : at + rows] = total
        at += rows

    @pl.when(group == pl.num_programs(0) - 1)
    def _():
        for sums, parts in ((raw_sum, RAW), (clipped_sum, CLIPPED)):
            at = 0
            for first, width in parts:
                together = LANES // width
                rows = columns // together
                turned = sums[at : at + rows].T
                for k in range(together):
                    here = (slice(first, first + width), slice(k * rows, (k + 1) * rows))
                    out_ref[here] = turned[k * width : (k + 1) * width] * scale + noise_ref[here]
                at += rows


def finish(raw, clipped, noise, scale):
    groups, examples, raw_rows, _ = raw.shape
    rows = clipped.shape[1]
    whole = pl.BlockSpec(noise.shape, lambda g: (0, 0))
    return pl.pallas_call(
        functools.partial(finish_kernel, scale),
        grid=(groups // TOGETHER,),
        in_specs=[
            pl.BlockSpec((TOGETHER, examples, raw_rows, LANES), lambda g: (g, 0, 0, 0)),
            pl.BlockSpec((TOGETHER, rows, LANES), lambda g: (g, 0, 0)),
            whole,
        ],
        out_specs=whole,
        out_shape=jax.ShapeDtypeStruct(noise.shape, jnp.float32),
        scratch_shapes=[pltpu.VMEM((raw_rows, LANES), jnp.float32), pltpu.VMEM((rows - EXTRA, LANES), jnp.float32)],
        compiler_params=PARAMS,
    )(raw, clipped, noise)


def per_device(activations, out_grads, lengths, clip_bound, noise):
    owners = lax.axis_size("dp")
    devices = lax.axis_size("tensor")
    examples = activations.shape[0]
    here = lax.axis_index("tensor")

    def along_z(x, k):
        return lax.ppermute(x, "tensor", [(t, (t + 2 * k) % devices) for t in range(devices)])

    def crossed(x, k):
        return lax.ppermute(x, "tensor", [(t, t ^ k) for t in range(devices)])

    own = part_features(activations, RAW)
    second = part_features(activations, CLIPPED)
    positions = lax.broadcasted_iota(jnp.int32, (1, out_grads.shape[1], 1), 1)
    masked = jnp.where(positions < lengths[:, None, None], out_grads, jnp.zeros_like(out_grads))
    masked = jnp.swapaxes(masked, 1, 2)

    up1, down1 = along_z(own, 1), along_z(own, -1)
    up1, down1, second = lax.optimization_barrier((up1, down1, second))
    second = lax.all_gather(second, "tensor")
    up2, down2 = along_z(up1, 1), along_z(down1, -1)
    up2, down2, masked = lax.optimization_barrier((up2, down2, masked))
    up3, down3 = along_z(up2, 1), along_z(down2, -1)
    up4, down4 = along_z(up3[:1], 1), along_z(down3[1:], -1)
    pieces = []
    for piece in (own, up1, down1, up2, down2, up3, down3):
        pieces += [piece, crossed(piece, 1)]
    pieces += [up4, crossed(up4, 1), down4, crossed(down4, 1)]
    step = jnp.array([2 * k for k in ARRIVALS for _ in range(2)], jnp.int32)
    second_core = jnp.array([0, 1] * len(ARRIVALS), jnp.int32)
    order = ((here & ~1) + step + ((here & 1) ^ second_core)) & (devices - 1)

    raw, exponents, squares = raw_products(order, pieces, masked)
    raw = lax.all_to_all(raw, "dp", 0, 0)
    products, share = plain_products(second, masked, squares)
    share = share + crossed(share, 1) + crossed(share, 2) + crossed(share, 3)
    share = share + crossed(share, 4) + crossed(share, 8) + crossed(share, 12)
    clipped = clipped_sums(clip_bound, share, products, exponents)
    clipped, raw = lax.optimization_barrier((clipped, raw))
    clipped = lax.all_to_all(clipped, "dp", 0, 0)
    return finish(raw, clipped, noise, float((examples * owners) ** -0.5))


def solution(mesh):
    in_specs = (P("dp", "tensor", None), P("dp", None, "tensor"), P("dp"), P(), P("dp", "tensor"))
    out_specs = P("dp", "tensor")
    return jax.shard_map(
        per_device, mesh=mesh, in_specs=in_specs, out_specs=out_specs, check_vma=False
    )
```

```python
import functools

import jax
import jax.numpy as jnp
from jax import lax
from jax.experimental import pallas as pl
from jax.experimental.pallas import tpu as pltpu
from jax.sharding import PartitionSpec as P

LANES = 128
EXTRA = 16
TOGETHER = 2
LEAST = 1e-33
PARAMS = pltpu.CompilerParams(vmem_limit_bytes=56 * 1024 * 1024)
LESS = pltpu.CompilerParams(vmem_limit_bytes=28 * 1024 * 1024)
RAW = ((0, 64), (64, 32))
CLIPPED = ((128, 128), (96, 32))
OWNED = sum(width for _, width in RAW + CLIPPED)
ARRIVALS = (0, -1, 1, -2, 2, -3, 3, 4)
SMALL = pl.CostEstimate(flops=1, bytes_accessed=1, transcendentals=0)


def part_kernel(parts, acts_ref, part_ref):
    at = 0
    for first, width in parts:
        for tile in range(acts_ref.shape[1] // OWNED * width // LANES):
            owners = range(tile * LANES // width, (tile + 1) * LANES // width)
            pieces = [acts_ref[:, o * OWNED + first : o * OWNED + first + width] for o in owners]
            part_ref[:, at : at + LANES] = jnp.concatenate(pieces, axis=1) if len(pieces) > 1 else pieces[0]
            at += LANES


def part_features(acts, parts):
    examples, shard, features = acts.shape
    taken = features // OWNED * sum(width for _, width in parts)
    return pl.pallas_call(
        functools.partial(part_kernel, parts),
        out_shape=jax.ShapeDtypeStruct((examples * shard, taken), acts.dtype),
        compiler_params=PARAMS,
    )(acts.reshape(examples * shard, features)).reshape(examples, shard, taken)


def tops(values):
    return jnp.max(jnp.abs(values), axis=0, keepdims=True)


def coded(values, top):
    exponent = jnp.ceil(jnp.log2(jnp.maximum(top, LEAST)) - 14.99)
    return jnp.round(values * jnp.exp2(-exponent)), exponent


def narrow(units):
    return units.astype(jnp.int32).astype(jnp.int16)


def packed(tile, owners):
    if owners == 1:
        return [tile]
    width, rows = LANES // owners, tile.shape[0] // owners
    lane = lax.broadcasted_iota(jnp.int32, (rows, LANES), 1)
    out = []
    for owner in range(owners):
        total = None
        for group in range(owners):
            piece = tile[group * rows : (group + 1) * rows]
            shift = (group - owner) * width % LANES
            piece = pltpu.roll(piece, shift, 1) if shift else piece
            total = piece if total is None else jnp.where(lane >= group * width, piece, total)
        out.append(total)
    return out


def packed_row(row, owners):
    return [t[0:1] for t in packed(jnp.broadcast_to(row, (8 * owners, LANES)), owners)]


def lane_sums(product):
    rows = jnp.sum(product * product, axis=0, keepdims=True)
    return sum(rows[:, at : at + LANES] for at in range(0, rows.shape[1], LANES))


def raw_kernel(order_ref, *refs):
    pieces, (grads_ref, coded_ref, exponent_ref, squares_ref, acts, grads, sems) = refs[:-7], refs[-7:]
    example = pl.program_id(0)
    depth = pieces[0].shape[1]

    def copies(e):
        far = pieces[-4 + 2 * e : len(pieces) - 2 + 2 * e]
        sources = [p.at[e] for p in pieces[:-4]] + [p.at[0] for p in far]
        made = [pltpu.make_async_copy(grads_ref.at[e], grads.at[e], sems.at[e, len(sources)])]
        for k, source in enumerate(sources):
            place = pl.ds(pl.multiple_of(order_ref[k] * depth, depth), depth)
            made.append(pltpu.make_async_copy(source, acts.at[e, place], sems.at[e, k]))
        return made

    @pl.when(example == 0)
    def _():
        for copy in copies(0) + copies(1):
            copy.start()
        for copy in copies(0):
            copy.wait()

    @pl.when(example == 1)
    def _():
        for copy in copies(1):
            copy.wait()

    product = jnp.dot(grads[example], acts[example], preferred_element_type=jnp.float32)
    squares_ref[0] = lane_sums(product)
    at = row = 0
    for h, (_, width) in enumerate(RAW):
        together = LANES // width
        rows = product.shape[0] // together
        for tile in range(coded_ref.shape[0] // together):
            tile_values = product[:, at : at + LANES]
            units, exponent = coded(tile_values, tops(tile_values))
            exponents = packed_row(exponent, together)
            for k, block in enumerate(packed(units, together)):
                coded_ref[tile * together + k, 0, row : row + rows] = narrow(block)
                exponent_ref[tile * together + k, 0, h : h + 1] = exponents[k]
            at += LANES
        row += rows


def raw_products(order, pieces, grads):
    examples, shard, features = pieces[0].shape
    _, columns, positions = grads.shape
    owners = features // sum(width for _, width in RAW)
    rows = columns * features // owners // LANES
    return pl.pallas_call(
        raw_kernel,
        grid=(examples,),
        in_specs=[pl.BlockSpec(memory_space=pltpu.SMEM)]
        + [pl.BlockSpec(memory_space=pltpu.HBM)] * (len(pieces) + 1),
        out_specs=[
            pl.BlockSpec((owners, 1, rows, LANES), lambda e: (0, e, 0, 0)),
            pl.BlockSpec((owners, 1, 8, LANES), lambda e: (0, e, 0, 0)),
            pl.BlockSpec((1, 1, LANES), lambda e: (e, 0, 0)),
        ],
        out_shape=[
            jax.ShapeDtypeStruct((owners, examples, rows, LANES), jnp.int16),
            jax.ShapeDtypeStruct((owners, examples, 8, LANES), jnp.float32),
            jax.ShapeDtypeStruct((examples, 1, LANES), jnp.float32),
        ],
        scratch_shapes=[
            pltpu.VMEM((examples, positions, features), pieces[0].dtype),
            pltpu.VMEM(grads.shape, grads.dtype),
            pltpu.SemaphoreType.DMA((examples, len(order) + 1)),
        ],
        compiler_params=PARAMS,
    )(order, *pieces, grads)


def plain_kernel(acts_ref, grads_ref, squares_ref, product_ref, top_ref, share_ref, acts, grads, acts_sems, grads_sems):
    devices, examples, shard, _ = acts_ref.shape
    width = product_ref.shape[2]
    tiles = acts_ref.shape[3] // width
    example, tile = pl.program_id(0), pl.program_id(1)

    def acts_copy(step):
        here = pl.ds(step % tiles * width, width)
        source = acts_ref.at[:, step // tiles, :, here]
        return pltpu.make_async_copy(source, acts.at[step % 2], acts_sems.at[step % 2])

    def grads_copy(e):
        return pltpu.make_async_copy(grads_ref.at[e], grads.at[e], grads_sems.at[e])

    for step in range(examples * tiles):

        @pl.when(example * tiles + tile == step)
        def _():
            if step == 0:
                acts_copy(0).start()
                for e in range(examples):
                    grads_copy(e).start()
            if step + 1 < examples * tiles:
                acts_copy(step + 1).start()
            acts_copy(step).wait()
            if step % tiles == 0:
                grads_copy(step // tiles).wait()
            rows = acts[step % 2].reshape(devices * shard, width)
            product_ref[0] = jnp.dot(grads[step // tiles], rows, preferred_element_type=jnp.float32)

    product = product_ref[0]
    top_ref[0] = tops(product)

    @pl.when(tile == 0)
    def _():
        share_ref[...] = squares_ref[...]

    share_ref[0] += lane_sums(product)


def plain_products(acts, grads, squares):
    devices, examples, shard, features = acts.shape
    _, columns, _ = grads.shape
    width = features // 2
    row = pl.BlockSpec((1, 1, LANES), lambda e, i: (e, 0, 0))
    hbm = pl.BlockSpec(memory_space=pltpu.HBM)
    return pl.pallas_call(
        plain_kernel,
        grid=(examples, features // width),
        in_specs=[hbm, hbm, row],
        out_specs=[
            pl.BlockSpec((1, columns, width), lambda e, i: (e, 0, i)),
            pl.BlockSpec((1, 1, width), lambda e, i: (e, 0, i)),
            row,
        ],
        out_shape=[
            jax.ShapeDtypeStruct((examples, columns, features), jnp.float32),
            jax.ShapeDtypeStruct((examples, 1, features), jnp.float32),
            jax.ShapeDtypeStruct((examples, 1, LANES), jnp.float32),
        ],
        scratch_shapes=[
            pltpu.VMEM((2, devices, shard, width), acts.dtype),
            pltpu.VMEM(grads.shape, grads.dtype),
            pltpu.SemaphoreType.DMA((2,)),
            pltpu.SemaphoreType.DMA((examples,)),
        ],
        cost_estimate=SMALL,
        compiler_params=LESS,
    )(*(pltpu.with_memory_space_constraint(a, pltpu.HBM) for a in (acts, grads, squares)))


def clipped_kernel(clip_ref, shares_ref, wide_ref, thin_ref, wide_top_ref, thin_top_ref, exponent_ref, coded_ref):
    examples, columns, _ = wide_ref.shape
    owners = coded_ref.shape[0]
    clip = clip_ref[0]
    blank = jnp.zeros((1, LANES), jnp.float32)
    wide, thin, wide_top, thin_top, extra = 0.0, 0.0, 0.0, 0.0, [[] for _ in range(owners)]
    for e in range(examples):
        square = jnp.sum(shares_ref[e], axis=1, keepdims=True)
        factor = clip / jnp.maximum(jnp.sqrt(square), clip)
        wide = wide + factor * wide_ref[e]
        thin = thin + factor * thin_ref[e]
        wide_top = wide_top + factor * wide_top_ref[e]
        thin_top = thin_top + factor * thin_top_ref[e]
        power = jnp.floor(jnp.log2(jnp.maximum(factor, LEAST))) + 1.0
        scaled = factor * jnp.exp2(-power) * 16384.0
        high = jnp.floor(scaled)
        low = jnp.round((scaled - high) * 16384.0)
        for k in range(owners):
            extra[k] += [blank + high, blank + low]
            extra[k] += [exponent_ref[k, e, h : h + 1] + power for h in range(len(RAW))]
    thin_units, exponent = coded(thin, thin_top)
    thin_units, thin_exponents = packed(thin_units, owners), packed_row(exponent, owners)
    for k in range(owners):
        here = slice(k * LANES, (k + 1) * LANES)
        units, exponent = coded(wide[:, here], wide_top[:, here])
        rows = extra[k] + [exponent, thin_exponents[k]]
        rows = jnp.concatenate(rows + [blank] * (EXTRA - len(rows)), axis=0)
        coded_ref[k, :columns] = narrow(units)
        coded_ref[k, columns : coded_ref.shape[1] - EXTRA] = narrow(thin_units[k])
        coded_ref[k, coded_ref.shape[1] - EXTRA :] = narrow(rows)


def clipped_sums(clip_bound, shares, products, top, exponents):
    examples, columns, features = products.shape
    owners = exponents.shape[0]
    together = LANES // CLIPPED[1][1]
    rows = columns * features // owners // LANES + EXTRA
    return pl.pallas_call(
        clipped_kernel,
        grid=(owners // together,),
        in_specs=[
            pl.BlockSpec(memory_space=pltpu.SMEM),
            pl.BlockSpec(shares.shape, lambda i: (0, 0, 0)),
            pl.BlockSpec((examples, columns, together * LANES), lambda i: (0, 0, i)),
            pl.BlockSpec((examples, columns, LANES), lambda i: (0, 0, owners + i)),
            pl.BlockSpec((examples, 1, together * LANES), lambda i: (0, 0, i)),
            pl.BlockSpec((examples, 1, LANES), lambda i: (0, 0, owners + i)),
            pl.BlockSpec((together, examples, 8, LANES), lambda i: (i, 0, 0, 0)),
        ],
        out_specs=pl.BlockSpec((together, rows, LANES), lambda i: (i, 0, 0)),
        out_shape=jax.ShapeDtypeStruct((owners, rows, LANES), jnp.int16),
        cost_estimate=SMALL,
        compiler_params=LESS,
    )(clip_bound, shares, products, products, top, top, exponents)


def finish_kernel(scale, raw_ref, clipped_ref, noise_ref, out_ref, raw_sum, clipped_sum):
    _, examples, _, _ = raw_ref.shape
    columns = out_ref.shape[1]
    group = pl.program_id(0)

    @pl.when(group == 0)
    def _():
        raw_sum[...] = jnp.zeros_like(raw_sum)
        clipped_sum[...] = jnp.zeros_like(clipped_sum)

    kinds = len(RAW)
    bottom = clipped_sum.shape[0]
    extra = [clipped_ref[g, bottom:].astype(jnp.float32) for g in range(TOGETHER)]
    at = 0
    for h, (_, width) in enumerate(RAW):
        rows = columns * width // LANES
        total = raw_sum[at : at + rows]
        for g in range(TOGETHER):
            row = lambda k: extra[g][k : k + 1]
            for e in range(examples):
                base = e * (2 + kinds)
                weight = (row(base) + row(base + 1) * (1.0 / 16384.0)) * (1.0 / 16384.0) * jnp.exp2(row(base + 2 + h))
                total = total + weight * raw_ref[g, e, at : at + rows].astype(jnp.float32)
        raw_sum[at : at + rows] = total
        at += rows
    at = 0
    for h, (_, width) in enumerate(CLIPPED):
        rows = columns * width // LANES
        total = clipped_sum[at : at + rows]
        for g in range(TOGETHER):
            k = examples * (2 + kinds) + h
            total = total + jnp.exp2(extra[g][k : k + 1]) * clipped_ref[g, at : at + rows].astype(jnp.float32)
        clipped_sum[at : at + rows] = total
        at += rows

    @pl.when(group == pl.num_programs(0) - 1)
    def _():
        for sums, parts in ((raw_sum, RAW), (clipped_sum, CLIPPED)):
            at = 0
            for first, width in parts:
                together = LANES // width
                rows = columns // together
                turned = sums[at : at + rows].T
                for k in range(together):
                    here = (slice(first, first + width), slice(k * rows, (k + 1) * rows))
                    out_ref[here] = turned[k * width : (k + 1) * width] * scale + noise_ref[here]
                at += rows


def finish(raw, clipped, noise, scale):
    groups, examples, raw_rows, _ = raw.shape
    rows = clipped.shape[1]
    whole = pl.BlockSpec(noise.shape, lambda g: (0, 0))
    return pl.pallas_call(
        functools.partial(finish_kernel, scale),
        grid=(groups // TOGETHER,),
        in_specs=[
            pl.BlockSpec((TOGETHER, examples, raw_rows, LANES), lambda g: (g, 0, 0, 0)),
            pl.BlockSpec((TOGETHER, rows, LANES), lambda g: (g, 0, 0)),
            whole,
        ],
        out_specs=whole,
        out_shape=jax.ShapeDtypeStruct(noise.shape, jnp.float32),
        scratch_shapes=[pltpu.VMEM((raw_rows, LANES), jnp.float32), pltpu.VMEM((rows - EXTRA, LANES), jnp.float32)],
        compiler_params=PARAMS,
    )(raw, clipped, noise)


def per_device(activations, out_grads, lengths, clip_bound, noise):
    owners = lax.axis_size("dp")
    devices = lax.axis_size("tensor")
    examples = activations.shape[0]
    here = lax.axis_index("tensor")

    def along_z(x, k):
        return lax.ppermute(x, "tensor", [(t, (t + 2 * k) % devices) for t in range(devices)])

    def crossed(x, k):
        return lax.ppermute(x, "tensor", [(t, t ^ k) for t in range(devices)])

    own = part_features(activations, RAW)
    second = part_features(activations, CLIPPED)
    positions = lax.broadcasted_iota(jnp.int32, (1, out_grads.shape[1], 1), 1)
    masked = jnp.where(positions < lengths[:, None, None], out_grads, jnp.zeros_like(out_grads))
    masked = jnp.swapaxes(masked, 1, 2)

    up1, down1 = along_z(own, 1), along_z(own, -1)
    up1, down1, second = lax.optimization_barrier((up1, down1, second))
    second = lax.all_gather(second, "tensor")
    up2, down2 = along_z(up1, 1), along_z(down1, -1)
    up2, down2, masked = lax.optimization_barrier((up2, down2, masked))
    up3, down3 = along_z(up2, 1), along_z(down2, -1)
    up4, down4 = along_z(up3[:1], 1), along_z(down3[1:], -1)
    pieces = []
    for piece in (own, up1, down1, up2, down2, up3, down3):
        pieces += [piece, crossed(piece, 1)]
    pieces += [up4, crossed(up4, 1), down4, crossed(down4, 1)]
    step = jnp.array([2 * k for k in ARRIVALS for _ in range(2)], jnp.int32)
    second_core = jnp.array([0, 1] * len(ARRIVALS), jnp.int32)
    order = ((here & ~1) + step + ((here & 1) ^ second_core)) & (devices - 1)

    raw, exponents, squares = raw_products(order, pieces, masked)
    raw = lax.all_to_all(raw, "dp", 0, 0)
    products, top, share = plain_products(second, masked, squares)
    share = share + crossed(share, 1) + crossed(share, 2) + crossed(share, 3)
    share = share + crossed(share, 4) + crossed(share, 8) + crossed(share, 12)
    clipped = clipped_sums(clip_bound, share, products, top, exponents)
    clipped, raw = lax.optimization_barrier((clipped, raw))
    clipped = lax.all_to_all(clipped, "dp", 0, 0)
    return finish(raw, clipped, noise, float((examples * owners) ** -0.5))


def solution(mesh):
    in_specs = (P("dp", "tensor", None), P("dp", None, "tensor"), P("dp"), P(), P("dp", "tensor"))
    out_specs = P("dp", "tensor")
    return jax.shard_map(
        per_device, mesh=mesh, in_specs=in_specs, out_specs=out_specs, check_vma=False
    )
```

```python
import functools

import jax
import jax.numpy as jnp
from jax import lax
from jax.experimental import pallas as pl
from jax.experimental.pallas import tpu as pltpu
from jax.sharding import PartitionSpec as P

LANES = 128
EXTRA = 16
TOGETHER = 4
LEAST = 1e-33
PARAMS = pltpu.CompilerParams(vmem_limit_bytes=56 * 1024 * 1024)
LESS = pltpu.CompilerParams(vmem_limit_bytes=28 * 1024 * 1024)
RAW = ((0, 64), (64, 32))
CLIPPED = ((128, 128), (96, 32))
OWNED = sum(width for _, width in RAW + CLIPPED)
ARRIVALS = (0, -1, 1, -2, 2, -3, 3, 4)
SMALL = pl.CostEstimate(flops=1, bytes_accessed=1, transcendentals=0)


def part_kernel(parts, acts_ref, part_ref):
    at = 0
    for first, width in parts:
        for tile in range(acts_ref.shape[1] // OWNED * width // LANES):
            owners = range(tile * LANES // width, (tile + 1) * LANES // width)
            pieces = [acts_ref[:, o * OWNED + first : o * OWNED + first + width] for o in owners]
            part_ref[:, at : at + LANES] = jnp.concatenate(pieces, axis=1) if len(pieces) > 1 else pieces[0]
            at += LANES


def part_features(acts, parts):
    examples, shard, features = acts.shape
    taken = features // OWNED * sum(width for _, width in parts)
    return pl.pallas_call(
        functools.partial(part_kernel, parts),
        grid=(examples,),
        in_specs=[pl.BlockSpec((shard, features), lambda e: (e, 0))],
        out_specs=pl.BlockSpec((shard, taken), lambda e: (e, 0)),
        out_shape=jax.ShapeDtypeStruct((examples * shard, taken), acts.dtype),
        compiler_params=PARAMS,
    )(acts.reshape(examples * shard, features)).reshape(examples, shard, taken)


def tops(values):
    return jnp.max(jnp.abs(values), axis=0, keepdims=True)


def coded(values, top):
    exponent = jnp.ceil(jnp.log2(jnp.maximum(top, LEAST)) - 14.99)
    return jnp.round(values * jnp.exp2(-exponent)), exponent


def narrow(units):
    return units.astype(jnp.int32).astype(jnp.int16)


def packed(tile, owners):
    if owners == 1:
        return [tile]
    width, rows = LANES // owners, tile.shape[0] // owners
    lane = lax.broadcasted_iota(jnp.int32, (rows, LANES), 1)
    out = []
    for owner in range(owners):
        total = None
        for group in range(owners):
            piece = tile[group * rows : (group + 1) * rows]
            shift = (group - owner) * width % LANES
            piece = pltpu.roll(piece, shift, 1) if shift else piece
            total = piece if total is None else jnp.where(lane >= group * width, piece, total)
        out.append(total)
    return out


def packed_row(row, owners):
    return [t[0:1] for t in packed(jnp.broadcast_to(row, (8 * owners, LANES)), owners)]


def lane_sums(product):
    rows = jnp.sum(product * product, axis=0, keepdims=True)
    return sum(rows[:, at : at + LANES] for at in range(0, rows.shape[1], LANES))


def raw_kernel(order_ref, *refs):
    pieces, (grads_ref, coded_ref, exponent_ref, squares_ref, acts, grads, sems) = refs[:-7], refs[-7:]
    example = pl.program_id(0)
    depth = pieces[0].shape[1]

    def copies(e):
        far = pieces[-4 + 2 * e : len(pieces) - 2 + 2 * e]
        sources = [p.at[e] for p in pieces[:-4]] + [p.at[0] for p in far]
        made = [pltpu.make_async_copy(grads_ref.at[e], grads.at[e], sems.at[e, len(sources)])]
        for k, source in enumerate(sources):
            place = pl.ds(pl.multiple_of(order_ref[k] * depth, depth), depth)
            made.append(pltpu.make_async_copy(source, acts.at[e, place], sems.at[e, k]))
        return made

    @pl.when(example == 0)
    def _():
        for copy in copies(0) + copies(1):
            copy.start()
        for copy in copies(0):
            copy.wait()

    @pl.when(example == 1)
    def _():
        for copy in copies(1):
            copy.wait()

    product = jnp.dot(grads[example], acts[example], preferred_element_type=jnp.float32)
    squares_ref[0] = lane_sums(product)
    at = row = 0
    for h, (_, width) in enumerate(RAW):
        together = LANES // width
        rows = product.shape[0] // together
        for tile in range(coded_ref.shape[0] // together):
            tile_values = product[:, at : at + LANES]
            units, exponent = coded(tile_values, tops(tile_values))
            exponents = packed_row(exponent, together)
            for k, block in enumerate(packed(units, together)):
                coded_ref[tile * together + k, 0, row : row + rows] = narrow(block)
                exponent_ref[tile * together + k, 0, h : h + 1] = exponents[k]
            at += LANES
        row += rows


def raw_products(order, pieces, grads):
    examples, shard, features = pieces[0].shape
    _, columns, positions = grads.shape
    owners = features // sum(width for _, width in RAW)
    rows = columns * features // owners // LANES
    return pl.pallas_call(
        raw_kernel,
        grid=(examples,),
        in_specs=[pl.BlockSpec(memory_space=pltpu.SMEM)]
        + [pl.BlockSpec(memory_space=pltpu.HBM)] * (len(pieces) + 1),
        out_specs=[
            pl.BlockSpec((owners, 1, rows, LANES), lambda e: (0, e, 0, 0)),
            pl.BlockSpec((owners, 1, 8, LANES), lambda e: (0, e, 0, 0)),
            pl.BlockSpec((1, 1, LANES), lambda e: (e, 0, 0)),
        ],
        out_shape=[
            jax.ShapeDtypeStruct((owners, examples, rows, LANES), jnp.int16),
            jax.ShapeDtypeStruct((owners, examples, 8, LANES), jnp.float32),
            jax.ShapeDtypeStruct((examples, 1, LANES), jnp.float32),
        ],
        scratch_shapes=[
            pltpu.VMEM((examples, positions, features), pieces[0].dtype),
            pltpu.VMEM(grads.shape, grads.dtype),
            pltpu.SemaphoreType.DMA((examples, len(order) + 1)),
        ],
        compiler_params=PARAMS,
    )(order, *pieces, grads)


def plain_kernel(acts_ref, grads_ref, squares_ref, product_ref, top_ref, share_ref, acts, grads, acts_sems, grads_sems):
    devices, examples, shard, _ = acts_ref.shape
    width = product_ref.shape[2]
    tiles = acts_ref.shape[3] // width
    example, tile = pl.program_id(0), pl.program_id(1)

    def acts_copy(step):
        here = pl.ds(step % tiles * width, width)
        source = acts_ref.at[:, step // tiles, :, here]
        return pltpu.make_async_copy(source, acts.at[step % 2], acts_sems.at[step % 2])

    def grads_copy(e):
        return pltpu.make_async_copy(grads_ref.at[e], grads.at[e], grads_sems.at[e])

    for step in range(examples * tiles):

        @pl.when(example * tiles + tile == step)
        def _():
            if step == 0:
                acts_copy(0).start()
                for e in range(examples):
                    grads_copy(e).start()
            if step + 1 < examples * tiles:
                acts_copy(step + 1).start()
            acts_copy(step).wait()
            if step % tiles == 0:
                grads_copy(step // tiles).wait()
            rows = acts[step % 2].reshape(devices * shard, width)
            product_ref[0] = jnp.dot(grads[step // tiles], rows, preferred_element_type=jnp.float32)

    product = product_ref[0]
    top_ref[0] = tops(product)

    @pl.when(tile == 0)
    def _():
        share_ref[...] = squares_ref[...]

    share_ref[0] += lane_sums(product)


def plain_products(acts, grads, squares):
    devices, examples, shard, features = acts.shape
    _, columns, _ = grads.shape
    width = features // 2
    row = pl.BlockSpec((1, 1, LANES), lambda e, i: (e, 0, 0))
    hbm = pl.BlockSpec(memory_space=pltpu.HBM)
    return pl.pallas_call(
        plain_kernel,
        grid=(examples, features // width),
        in_specs=[hbm, hbm, row],
        out_specs=[
            pl.BlockSpec((1, columns, width), lambda e, i: (e, 0, i)),
            pl.BlockSpec((1, 1, width), lambda e, i: (e, 0, i)),
            row,
        ],
        out_shape=[
            jax.ShapeDtypeStruct((examples, columns, features), jnp.float32),
            jax.ShapeDtypeStruct((examples, 1, features), jnp.float32),
            jax.ShapeDtypeStruct((examples, 1, LANES), jnp.float32),
        ],
        scratch_shapes=[
            pltpu.VMEM((2, devices, shard, width), acts.dtype),
            pltpu.VMEM(grads.shape, grads.dtype),
            pltpu.SemaphoreType.DMA((2,)),
            pltpu.SemaphoreType.DMA((examples,)),
        ],
        cost_estimate=SMALL,
        compiler_params=LESS,
    )(*(pltpu.with_memory_space_constraint(a, pltpu.HBM) for a in (acts, grads, squares)))


def clipped_kernel(clip_ref, shares_ref, wide_ref, thin_ref, wide_top_ref, thin_top_ref, exponent_ref, coded_ref):
    examples, columns, _ = wide_ref.shape
    owners = coded_ref.shape[0]
    clip = clip_ref[0]
    blank = jnp.zeros((1, LANES), jnp.float32)
    wide, thin, wide_top, thin_top, extra = 0.0, 0.0, 0.0, 0.0, [[] for _ in range(owners)]
    for e in range(examples):
        square = jnp.sum(shares_ref[e], axis=1, keepdims=True)
        factor = clip / jnp.maximum(jnp.sqrt(square), clip)
        wide = wide + factor * wide_ref[e]
        thin = thin + factor * thin_ref[e]
        wide_top = wide_top + factor * wide_top_ref[e]
        thin_top = thin_top + factor * thin_top_ref[e]
        power = jnp.floor(jnp.log2(jnp.maximum(factor, LEAST))) + 1.0
        scaled = factor * jnp.exp2(-power) * 16384.0
        high = jnp.floor(scaled)
        low = jnp.round((scaled - high) * 16384.0)
        for k in range(owners):
            extra[k] += [blank + high, blank + low]
            extra[k] += [exponent_ref[k, e, h : h + 1] + power for h in range(len(RAW))]
    thin_units, exponent = coded(thin, thin_top)
    thin_units, thin_exponents = packed(thin_units, owners), packed_row(exponent, owners)
    for k in range(owners):
        here = slice(k * LANES, (k + 1) * LANES)
        units, exponent = coded(wide[:, here], wide_top[:, here])
        rows = extra[k] + [exponent, thin_exponents[k]]
        rows = jnp.concatenate(rows + [blank] * (EXTRA - len(rows)), axis=0)
        coded_ref[k, :columns] = narrow(units)
        coded_ref[k, columns : coded_ref.shape[1] - EXTRA] = narrow(thin_units[k])
        coded_ref[k, coded_ref.shape[1] - EXTRA :] = narrow(rows)


def clipped_sums(clip_bound, shares, products, top, exponents):
    examples, columns, features = products.shape
    owners = exponents.shape[0]
    together = LANES // CLIPPED[1][1]
    rows = columns * features // owners // LANES + EXTRA
    return pl.pallas_call(
        clipped_kernel,
        grid=(owners // together,),
        in_specs=[
            pl.BlockSpec(memory_space=pltpu.SMEM),
            pl.BlockSpec(shares.shape, lambda i: (0, 0, 0)),
            pl.BlockSpec((examples, columns, together * LANES), lambda i: (0, 0, i)),
            pl.BlockSpec((examples, columns, LANES), lambda i: (0, 0, owners + i)),
            pl.BlockSpec((examples, 1, together * LANES), lambda i: (0, 0, i)),
            pl.BlockSpec((examples, 1, LANES), lambda i: (0, 0, owners + i)),
            pl.BlockSpec((together, examples, 8, LANES), lambda i: (i, 0, 0, 0)),
        ],
        out_specs=pl.BlockSpec((together, rows, LANES), lambda i: (i, 0, 0)),
        out_shape=jax.ShapeDtypeStruct((owners, rows, LANES), jnp.int16),
        cost_estimate=SMALL,
        compiler_params=LESS,
    )(clip_bound, shares, products, products, top, top, exponents)


def finish_kernel(scale, raw_ref, clipped_ref, noise_ref, out_ref, raw_sum, clipped_sum):
    _, examples, _, _ = raw_ref.shape
    columns = out_ref.shape[1]
    group = pl.program_id(0)

    @pl.when(group == 0)
    def _():
        raw_sum[...] = jnp.zeros_like(raw_sum)
        clipped_sum[...] = jnp.zeros_like(clipped_sum)

    kinds = len(RAW)
    bottom = clipped_sum.shape[0]
    extra = [clipped_ref[g, bottom:].astype(jnp.float32) for g in range(TOGETHER)]
    at = 0
    for h, (_, width) in enumerate(RAW):
        rows = columns * width // LANES
        total = raw_sum[at : at + rows]
        for g in range(TOGETHER):
            row = lambda k: extra[g][k : k + 1]
            for e in range(examples):
                base = e * (2 + kinds)
                weight = (row(base) + row(base + 1) * (1.0 / 16384.0)) * (1.0 / 16384.0) * jnp.exp2(row(base + 2 + h))
                total = total + weight * raw_ref[g, e, at : at + rows].astype(jnp.float32)
        raw_sum[at : at + rows] = total
        at += rows
    at = 0
    for h, (_, width) in enumerate(CLIPPED):
        rows = columns * width // LANES
        total = clipped_sum[at : at + rows]
        for g in range(TOGETHER):
            k = examples * (2 + kinds) + h
            total = total + jnp.exp2(extra[g][k : k + 1]) * clipped_ref[g, at : at + rows].astype(jnp.float32)
        clipped_sum[at : at + rows] = total
        at += rows

    @pl.when(group == pl.num_programs(0) - 1)
    def _():
        for sums, parts in ((raw_sum, RAW), (clipped_sum, CLIPPED)):
            at = 0
            for first, width in parts:
                together = LANES // width
                rows = columns // together
                turned = sums[at : at + rows].T
                for k in range(together):
                    here = (slice(first, first + width), slice(k * rows, (k + 1) * rows))
                    out_ref[here] = turned[k * width : (k + 1) * width] * scale + noise_ref[here]
                at += rows


def finish(raw, clipped, noise, scale):
    groups, examples, raw_rows, _ = raw.shape
    rows = clipped.shape[1]
    whole = pl.BlockSpec(noise.shape, lambda g: (0, 0))
    return pl.pallas_call(
        functools.partial(finish_kernel, scale),
        grid=(groups // TOGETHER,),
        in_specs=[
            pl.BlockSpec((TOGETHER, examples, raw_rows, LANES), lambda g: (g, 0, 0, 0)),
            pl.BlockSpec((TOGETHER, rows, LANES), lambda g: (g, 0, 0)),
            whole,
        ],
        out_specs=whole,
        out_shape=jax.ShapeDtypeStruct(noise.shape, jnp.float32),
        scratch_shapes=[pltpu.VMEM((raw_rows, LANES), jnp.float32), pltpu.VMEM((rows - EXTRA, LANES), jnp.float32)],
        compiler_params=PARAMS,
    )(raw, clipped, noise)


def per_device(activations, out_grads, lengths, clip_bound, noise):
    owners = lax.axis_size("dp")
    devices = lax.axis_size("tensor")
    examples = activations.shape[0]
    here = lax.axis_index("tensor")

    def along_z(x, k):
        return lax.ppermute(x, "tensor", [(t, (t + 2 * k) % devices) for t in range(devices)])

    def crossed(x, k):
        return lax.ppermute(x, "tensor", [(t, t ^ k) for t in range(devices)])

    own = part_features(activations, RAW)
    second = part_features(activations, CLIPPED)
    positions = lax.broadcasted_iota(jnp.int32, (1, out_grads.shape[1], 1), 1)
    masked = jnp.where(positions < lengths[:, None, None], out_grads, jnp.zeros_like(out_grads))
    masked = jnp.swapaxes(masked, 1, 2)

    step = jnp.array([2 * k for k in ARRIVALS for _ in range(2)], jnp.int32)
    second_core = jnp.array([0, 1] * len(ARRIVALS), jnp.int32)
    order = ((here & ~1) + step + ((here & 1) ^ second_core)) & (devices - 1)

    up1, down1 = along_z(own, 1), along_z(own, -1)
    up2, down2 = along_z(up1, 1), along_z(down1, -1)
    up2, down2, second, masked, order = lax.optimization_barrier((up2, down2, second, masked, order))
    second = lax.all_gather(second, "tensor")
    up3, down3 = along_z(up2, 1), along_z(down2, -1)
    up4, down4 = along_z(up3[:1], 1), along_z(down3[1:], -1)
    pieces = []
    for piece in (own, up1, down1, up2, down2, up3, down3):
        pieces += [piece, crossed(piece, 1)]
    pieces += [up4, crossed(up4, 1), down4, crossed(down4, 1)]

    raw, exponents, squares = raw_products(order, pieces, masked)
    raw = lax.all_to_all(raw, "dp", 0, 0)
    products, top, share = plain_products(second, masked, squares)
    share = share + crossed(share, 1) + crossed(share, 2) + crossed(share, 3)
    share = share + crossed(share, 4) + crossed(share, 8) + crossed(share, 12)
    clipped = clipped_sums(clip_bound, share, products, top, exponents)
    clipped, raw = lax.optimization_barrier((clipped, raw))
    clipped = lax.all_to_all(clipped, "dp", 0, 0)
    return finish(raw, clipped, noise, float((examples * owners) ** -0.5))


def solution(mesh):
    in_specs = (P("dp", "tensor", None), P("dp", None, "tensor"), P("dp"), P(), P("dp", "tensor"))
    out_specs = P("dp", "tensor")
    return jax.shard_map(
        per_device, mesh=mesh, in_specs=in_specs, out_specs=out_specs, check_vma=False
    )
```

```python
import functools

import jax
import jax.numpy as jnp
from jax import lax
from jax.experimental import pallas as pl
from jax.experimental.pallas import tpu as pltpu
from jax.sharding import PartitionSpec as P

LANES = 128
EXTRA = 16
TOGETHER = 4
LEAST = 1e-33
CHUNK = 256
ROUND = 12582912.0
PARAMS = pltpu.CompilerParams(vmem_limit_bytes=56 * 1024 * 1024)
LESS = pltpu.CompilerParams(vmem_limit_bytes=28 * 1024 * 1024)
RAW = ((0, 64), (64, 32))
CLIPPED = ((128, 128), (96, 32))
OWNED = sum(width for _, width in RAW + CLIPPED)
ARRIVALS = (0, -1, 1, -2, 2, -3, 3, 4)
SMALL = pl.CostEstimate(flops=1, bytes_accessed=1, transcendentals=0)


def part_kernel(parts, acts_ref, part_ref):
    at = 0
    for first, width in parts:
        for tile in range(acts_ref.shape[1] // OWNED * width // LANES):
            owners = range(tile * LANES // width, (tile + 1) * LANES // width)
            pieces = [acts_ref[:, o * OWNED + first : o * OWNED + first + width] for o in owners]
            part_ref[:, at : at + LANES] = jnp.concatenate(pieces, axis=1) if len(pieces) > 1 else pieces[0]
            at += LANES


def part_features(acts, parts):
    examples, shard, features = acts.shape
    taken = features // OWNED * sum(width for _, width in parts)
    return pl.pallas_call(
        functools.partial(part_kernel, parts),
        grid=(examples,),
        in_specs=[pl.BlockSpec((shard, features), lambda e: (e, 0))],
        out_specs=pl.BlockSpec((shard, taken), lambda e: (e, 0)),
        out_shape=jax.ShapeDtypeStruct((examples * shard, taken), acts.dtype),
        compiler_params=PARAMS,
    )(acts.reshape(examples * shard, features)).reshape(examples, shard, taken)


def tops(values):
    return jnp.max(jnp.abs(values), axis=0, keepdims=True)


def coded(values, top):
    exponent = jnp.ceil(jnp.log2(jnp.maximum(top, LEAST)) - 14.99)
    return (values * jnp.exp2(-exponent) + ROUND) - ROUND, exponent


def narrow(units):
    return units.astype(jnp.int32).astype(jnp.int16)


def packed(tile, owners):
    if owners == 1:
        return [tile]
    width, rows = LANES // owners, tile.shape[0] // owners
    lane = lax.broadcasted_iota(jnp.int32, (rows, LANES), 1)
    out = []
    for owner in range(owners):
        total = None
        for group in range(owners):
            piece = tile[group * rows : (group + 1) * rows]
            shift = (group - owner) * width % LANES
            piece = pltpu.roll(piece, shift, 1) if shift else piece
            total = piece if total is None else jnp.where(lane >= group * width, piece, total)
        out.append(total)
    return out


def packed_row(row, owners):
    return [t[0:1] for t in packed(jnp.broadcast_to(row, (8 * owners, LANES)), owners)]


def lane_sums(product):
    rows = jnp.sum(product * product, axis=0, keepdims=True)
    return sum(rows[:, at : at + LANES] for at in range(0, rows.shape[1], LANES))


def raw_kernel(order_ref, *refs):
    pieces, (grads_ref, coded_ref, exponent_ref, squares_ref, acts, grads, sems) = refs[:-7], refs[-7:]
    example = pl.program_id(0)
    depth = pieces[0].shape[1]

    def copies(e):
        far = pieces[-4 + 2 * e : len(pieces) - 2 + 2 * e]
        sources = [p.at[e] for p in pieces[:-4]] + [p.at[0] for p in far]
        made = [pltpu.make_async_copy(grads_ref.at[e], grads.at[e], sems.at[e, len(sources)])]
        for k, source in enumerate(sources):
            place = pl.ds(pl.multiple_of(order_ref[k] * depth, depth), depth)
            made.append(pltpu.make_async_copy(source, acts.at[e, place], sems.at[e, k]))
        return made

    @pl.when(example == 0)
    def _():
        for copy in copies(0) + copies(1):
            copy.start()
        for copy in copies(0):
            copy.wait()

    @pl.when(example == 1)
    def _():
        for copy in copies(1):
            copy.wait()

    columns = grads.shape[1]
    squares = jnp.zeros((1, LANES), jnp.float32)
    at = row = 0
    for h, (_, width) in enumerate(RAW):
        together = LANES // width
        rows = columns // together
        for tile in range(coded_ref.shape[0] // together):
            if at % CHUNK == 0:
                some = acts[example, :, at : at + CHUNK]
                product = jnp.dot(grads[example], some, preferred_element_type=jnp.float32)
                squares = squares + lane_sums(product)
            values = product[:, at % CHUNK : at % CHUNK + LANES]
            units, exponent = coded(values, tops(values))
            exponents = packed_row(exponent, together)
            for k, block in enumerate(packed(units, together)):
                coded_ref[tile * together + k, 0, row : row + rows] = narrow(block)
                exponent_ref[tile * together + k, 0, h : h + 1] = exponents[k]
            at += LANES
        row += rows
    squares_ref[0] = squares


def raw_products(order, pieces, grads):
    examples, shard, features = pieces[0].shape
    _, columns, positions = grads.shape
    owners = features // sum(width for _, width in RAW)
    rows = columns * features // owners // LANES
    return pl.pallas_call(
        raw_kernel,
        grid=(examples,),
        in_specs=[pl.BlockSpec(memory_space=pltpu.SMEM)]
        + [pl.BlockSpec(memory_space=pltpu.HBM)] * (len(pieces) + 1),
        out_specs=[
            pl.BlockSpec((owners, 1, rows, LANES), lambda e: (0, e, 0, 0)),
            pl.BlockSpec((owners, 1, 8, LANES), lambda e: (0, e, 0, 0)),
            pl.BlockSpec((1, 1, LANES), lambda e: (e, 0, 0)),
        ],
        out_shape=[
            jax.ShapeDtypeStruct((owners, examples, rows, LANES), jnp.int16),
            jax.ShapeDtypeStruct((owners, examples, 8, LANES), jnp.float32),
            jax.ShapeDtypeStruct((examples, 1, LANES), jnp.float32),
        ],
        scratch_shapes=[
            pltpu.VMEM((examples, positions, features), pieces[0].dtype),
            pltpu.VMEM(grads.shape, grads.dtype),
            pltpu.SemaphoreType.DMA((examples, len(order) + 1)),
        ],
        compiler_params=PARAMS,
    )(order, *pieces, grads)


def plain_kernel(acts_ref, grads_ref, squares_ref, product_ref, top_ref, share_ref, acts, grads, acts_sems, grads_sems):
    devices, examples, shard, _ = acts_ref.shape
    width = product_ref.shape[2]
    tiles = acts_ref.shape[3] // width
    example, tile = pl.program_id(0), pl.program_id(1)

    def acts_copy(step):
        here = pl.ds(step % tiles * width, width)
        source = acts_ref.at[:, step // tiles, :, here]
        return pltpu.make_async_copy(source, acts.at[step % 2], acts_sems.at[step % 2])

    def grads_copy(e):
        return pltpu.make_async_copy(grads_ref.at[e], grads.at[e], grads_sems.at[e])

    for step in range(examples * tiles):

        @pl.when(example * tiles + tile == step)
        def _():
            if step == 0:
                acts_copy(0).start()
                for e in range(examples):
                    grads_copy(e).start()
            if step + 1 < examples * tiles:
                acts_copy(step + 1).start()
            acts_copy(step).wait()
            if step % tiles == 0:
                grads_copy(step // tiles).wait()

    @pl.when(tile == 0)
    def _():
        share_ref[...] = squares_ref[...]

    slot = (example * tiles + tile) % 2
    share = share_ref[0]
    for at in range(0, width, CHUNK):
        here = slice(at, at + CHUNK)
        some = acts[slot, :, :, here].reshape(devices * shard, CHUNK)
        product = jnp.dot(grads[example], some, preferred_element_type=jnp.float32)
        product_ref[0, :, here] = product
        top_ref[0, :, here] = tops(product)
        share = share + lane_sums(product)
    share_ref[0] = share


def plain_products(acts, grads, squares):
    devices, examples, shard, features = acts.shape
    _, columns, _ = grads.shape
    width = features // 2
    row = pl.BlockSpec((1, 1, LANES), lambda e, i: (e, 0, 0))
    hbm = pl.BlockSpec(memory_space=pltpu.HBM)
    return pl.pallas_call(
        plain_kernel,
        grid=(examples, features // width),
        in_specs=[hbm, hbm, row],
        out_specs=[
            pl.BlockSpec((1, columns, width), lambda e, i: (e, 0, i)),
            pl.BlockSpec((1, 1, width), lambda e, i: (e, 0, i)),
            row,
        ],
        out_shape=[
            jax.ShapeDtypeStruct((examples, columns, features), jnp.float32),
            jax.ShapeDtypeStruct((examples, 1, features), jnp.float32),
            jax.ShapeDtypeStruct((examples, 1, LANES), jnp.float32),
        ],
        scratch_shapes=[
            pltpu.VMEM((2, devices, shard, width), acts.dtype),
            pltpu.VMEM(grads.shape, grads.dtype),
            pltpu.SemaphoreType.DMA((2,)),
            pltpu.SemaphoreType.DMA((examples,)),
        ],
        cost_estimate=SMALL,
        compiler_params=LESS,
    )(*(pltpu.with_memory_space_constraint(a, pltpu.HBM) for a in (acts, grads, squares)))


def clipped_kernel(clip_ref, shares_ref, wide_ref, thin_ref, wide_top_ref, thin_top_ref, exponent_ref, coded_ref):
    examples, columns, _ = wide_ref.shape
    owners = coded_ref.shape[0]
    clip = clip_ref[0]
    blank = jnp.zeros((1, LANES), jnp.float32)
    wide, thin, wide_top, thin_top, extra = 0.0, 0.0, 0.0, 0.0, [[] for _ in range(owners)]
    for e in range(examples):
        square = jnp.sum(shares_ref[e], axis=1, keepdims=True)
        factor = clip / jnp.maximum(jnp.sqrt(square), clip)
        wide = wide + factor * wide_ref[e]
        thin = thin + factor * thin_ref[e]
        wide_top = wide_top + factor * wide_top_ref[e]
        thin_top = thin_top + factor * thin_top_ref[e]
        power = jnp.floor(jnp.log2(jnp.maximum(factor, LEAST))) + 1.0
        scaled = factor * jnp.exp2(-power) * 16384.0
        high = jnp.floor(scaled)
        low = jnp.round((scaled - high) * 16384.0)
        for k in range(owners):
            extra[k] += [blank + high, blank + low]
            extra[k] += [exponent_ref[k, e, h : h + 1] + power for h in range(len(RAW))]
    thin_units, exponent = coded(thin, thin_top)
    thin_units, thin_exponents = packed(thin_units, owners), packed_row(exponent, owners)
    for k in range(owners):
        here = slice(k * LANES, (k + 1) * LANES)
        units, exponent = coded(wide[:, here], wide_top[:, here])
        rows = extra[k] + [exponent, thin_exponents[k]]
        rows = jnp.concatenate(rows + [blank] * (EXTRA - len(rows)), axis=0)
        coded_ref[k, :columns] = narrow(units)
        coded_ref[k, columns : coded_ref.shape[1] - EXTRA] = narrow(thin_units[k])
        coded_ref[k, coded_ref.shape[1] - EXTRA :] = narrow(rows)


def clipped_sums(clip_bound, shares, products, top, exponents):
    examples, columns, features = products.shape
    owners = exponents.shape[0]
    together = LANES // CLIPPED[1][1]
    rows = columns * features // owners // LANES + EXTRA
    return pl.pallas_call(
        clipped_kernel,
        grid=(owners // together,),
        in_specs=[
            pl.BlockSpec(memory_space=pltpu.SMEM),
            pl.BlockSpec(shares.shape, lambda i: (0, 0, 0)),
            pl.BlockSpec((examples, columns, together * LANES), lambda i: (0, 0, i)),
            pl.BlockSpec((examples, columns, LANES), lambda i: (0, 0, owners + i)),
            pl.BlockSpec((examples, 1, together * LANES), lambda i: (0, 0, i)),
            pl.BlockSpec((examples, 1, LANES), lambda i: (0, 0, owners + i)),
            pl.BlockSpec((together, examples, 8, LANES), lambda i: (i, 0, 0, 0)),
        ],
        out_specs=pl.BlockSpec((together, rows, LANES), lambda i: (i, 0, 0)),
        out_shape=jax.ShapeDtypeStruct((owners, rows, LANES), jnp.int16),
        cost_estimate=SMALL,
        compiler_params=LESS,
    )(clip_bound, shares, products, products, top, top, exponents)


def finish_kernel(scale, raw_ref, clipped_ref, noise_ref, out_ref, raw_sum, clipped_sum):
    _, examples, _, _ = raw_ref.shape
    columns = out_ref.shape[1]
    group = pl.program_id(0)

    @pl.when(group == 0)
    def _():
        raw_sum[...] = jnp.zeros_like(raw_sum)
        clipped_sum[...] = jnp.zeros_like(clipped_sum)

    kinds = len(RAW)
    bottom = clipped_sum.shape[0]
    extra = [clipped_ref[g, bottom:].astype(jnp.float32) for g in range(TOGETHER)]
    at = 0
    for h, (_, width) in enumerate(RAW):
        rows = columns * width // LANES
        total = raw_sum[at : at + rows]
        for g in range(TOGETHER):
            row = lambda k: extra[g][k : k + 1]
            for e in range(examples):
                base = e * (2 + kinds)
                weight = (row(base) + row(base + 1) * (1.0 / 16384.0)) * (1.0 / 16384.0) * jnp.exp2(row(base + 2 + h))
                total = total + weight * raw_ref[g, e, at : at + rows].astype(jnp.float32)
        raw_sum[at : at + rows] = total
        at += rows
    at = 0
    for h, (_, width) in enumerate(CLIPPED):
        rows = columns * width // LANES
        total = clipped_sum[at : at + rows]
        for g in range(TOGETHER):
            k = examples * (2 + kinds) + h
            total = total + jnp.exp2(extra[g][k : k + 1]) * clipped_ref[g, at : at + rows].astype(jnp.float32)
        clipped_sum[at : at + rows] = total
        at += rows

    @pl.when(group == pl.num_programs(0) - 1)
    def _():
        for sums, parts in ((raw_sum, RAW), (clipped_sum, CLIPPED)):
            at = 0
            for first, width in parts:
                together = LANES // width
                rows = columns // together
                turned = sums[at : at + rows].T
                for k in range(together):
                    here = (slice(first, first + width), slice(k * rows, (k + 1) * rows))
                    out_ref[here] = turned[k * width : (k + 1) * width] * scale + noise_ref[here]
                at += rows


def finish(raw, clipped, noise, scale):
    groups, examples, raw_rows, _ = raw.shape
    rows = clipped.shape[1]
    whole = pl.BlockSpec(noise.shape, lambda g: (0, 0))
    return pl.pallas_call(
        functools.partial(finish_kernel, scale),
        grid=(groups // TOGETHER,),
        in_specs=[
            pl.BlockSpec((TOGETHER, examples, raw_rows, LANES), lambda g: (g, 0, 0, 0)),
            pl.BlockSpec((TOGETHER, rows, LANES), lambda g: (g, 0, 0)),
            whole,
        ],
        out_specs=whole,
        out_shape=jax.ShapeDtypeStruct(noise.shape, jnp.float32),
        scratch_shapes=[pltpu.VMEM((raw_rows, LANES), jnp.float32), pltpu.VMEM((rows - EXTRA, LANES), jnp.float32)],
        compiler_params=PARAMS,
    )(raw, clipped, noise)


def per_device(activations, out_grads, lengths, clip_bound, noise):
    owners = lax.axis_size("dp")
    devices = lax.axis_size("tensor")
    examples = activations.shape[0]
    here = lax.axis_index("tensor")

    def along_z(x, k):
        return lax.ppermute(x, "tensor", [(t, (t + 2 * k) % devices) for t in range(devices)])

    def crossed(x, k):
        return lax.ppermute(x, "tensor", [(t, t ^ k) for t in range(devices)])

    own = part_features(activations, RAW)
    second = part_features(activations, CLIPPED)
    positions = lax.broadcasted_iota(jnp.int32, (1, out_grads.shape[1], 1), 1)
    masked = jnp.where(positions < lengths[:, None, None], out_grads, jnp.zeros_like(out_grads))
    masked = jnp.swapaxes(masked, 1, 2)

    step = jnp.array([2 * k for k in ARRIVALS for _ in range(2)], jnp.int32)
    second_core = jnp.array([0, 1] * len(ARRIVALS), jnp.int32)
    order = ((here & ~1) + step + ((here & 1) ^ second_core)) & (devices - 1)

    up1, down1 = along_z(own, 1), along_z(own, -1)
    up2, down2 = along_z(up1, 1), along_z(down1, -1)
    up2, down2, second, masked, order = lax.optimization_barrier((up2, down2, second, masked, order))
    second = lax.all_gather(second, "tensor")
    up3, down3 = along_z(up2, 1), along_z(down2, -1)
    up4, down4 = along_z(up3[:1], 1), along_z(down3[1:], -1)
    pieces = []
    for piece in (own, up1, down1, up2, down2, up3, down3):
        pieces += [piece, crossed(piece, 1)]
    pieces += [up4, crossed(up4, 1), down4, crossed(down4, 1)]

    raw, exponents, squares = raw_products(order, pieces, masked)
    raw = lax.all_to_all(raw, "dp", 0, 0)
    products, top, share = plain_products(second, masked, squares)
    share = share + crossed(share, 1) + crossed(share, 2) + crossed(share, 3)
    share = share + crossed(share, 4) + crossed(share, 8) + crossed(share, 12)
    clipped = clipped_sums(clip_bound, share, products, top, exponents)
    clipped, raw = lax.optimization_barrier((clipped, raw))
    clipped = lax.all_to_all(clipped, "dp", 0, 0)
    return finish(raw, clipped, noise, float((examples * owners) ** -0.5))


def solution(mesh):
    in_specs = (P("dp", "tensor", None), P("dp", None, "tensor"), P("dp"), P(), P("dp", "tensor"))
    out_specs = P("dp", "tensor")
    return jax.shard_map(
        per_device, mesh=mesh, in_specs=in_specs, out_specs=out_specs, check_vma=False
    )
```

```python
import functools

import jax
import jax.numpy as jnp
from jax import lax
from jax.experimental import pallas as pl
from jax.experimental.pallas import tpu as pltpu
from jax.sharding import PartitionSpec as P

LANES = 128
EXTRA = 16
TOGETHER = 4
LEAST = 1e-33
CHUNK = 256
PARAMS = pltpu.CompilerParams(vmem_limit_bytes=56 * 1024 * 1024)
LESS = pltpu.CompilerParams(vmem_limit_bytes=28 * 1024 * 1024)
RAW = ((0, 64), (64, 32))
CLIPPED = ((128, 128), (96, 32))
OWNED = sum(width for _, width in RAW + CLIPPED)
ARRIVALS = (0, -1, 1, -2, 2, -3, 3, 4)
SMALL = pl.CostEstimate(flops=1, bytes_accessed=1, transcendentals=0)


def part_kernel(parts, acts_ref, part_ref):
    at = 0
    for first, width in parts:
        for tile in range(acts_ref.shape[1] // OWNED * width // LANES):
            owners = range(tile * LANES // width, (tile + 1) * LANES // width)
            pieces = [acts_ref[:, o * OWNED + first : o * OWNED + first + width] for o in owners]
            part_ref[:, at : at + LANES] = jnp.concatenate(pieces, axis=1) if len(pieces) > 1 else pieces[0]
            at += LANES


def part_features(acts, parts):
    examples, shard, features = acts.shape
    taken = features // OWNED * sum(width for _, width in parts)
    return pl.pallas_call(
        functools.partial(part_kernel, parts),
        grid=(examples,),
        in_specs=[pl.BlockSpec((shard, features), lambda e: (e, 0))],
        out_specs=pl.BlockSpec((shard, taken), lambda e: (e, 0)),
        out_shape=jax.ShapeDtypeStruct((examples * shard, taken), acts.dtype),
        compiler_params=PARAMS,
    )(acts.reshape(examples * shard, features)).reshape(examples, shard, taken)


def tops(values):
    return jnp.max(jnp.abs(values), axis=0, keepdims=True)


def coded(values, top):
    exponent = jnp.ceil(jnp.log2(jnp.maximum(top, LEAST)) - 14.99)
    return jnp.round(values * jnp.exp2(-exponent)), exponent


def narrow(units):
    return units.astype(jnp.int32).astype(jnp.int16)


def packed(tile, owners):
    if owners == 1:
        return [tile]
    width, rows = LANES // owners, tile.shape[0] // owners
    lane = lax.broadcasted_iota(jnp.int32, (rows, LANES), 1)
    out = []
    for owner in range(owners):
        total = None
        for group in range(owners):
            piece = tile[group * rows : (group + 1) * rows]
            shift = (group - owner) * width % LANES
            piece = pltpu.roll(piece, shift, 1) if shift else piece
            total = piece if total is None else jnp.where(lane >= group * width, piece, total)
        out.append(total)
    return out


def packed_row(row, owners):
    return [t[0:1] for t in packed(jnp.broadcast_to(row, (8 * owners, LANES)), owners)]


def lane_sums(product):
    rows = jnp.sum(product * product, axis=0, keepdims=True)
    return sum(rows[:, at : at + LANES] for at in range(0, rows.shape[1], LANES))


def raw_kernel(order_ref, *refs):
    pieces, (grads_ref, coded_ref, exponent_ref, squares_ref, acts, grads, sems) = refs[:-7], refs[-7:]
    example = pl.program_id(0)
    depth = pieces[0].shape[1]

    def copies(e):
        far = pieces[-4 + 2 * e : len(pieces) - 2 + 2 * e]
        sources = [p.at[e] for p in pieces[:-4]] + [p.at[0] for p in far]
        made = [pltpu.make_async_copy(grads_ref.at[e], grads.at[e], sems.at[e, len(sources)])]
        for k, source in enumerate(sources):
            place = pl.ds(pl.multiple_of(order_ref[k] * depth, depth), depth)
            made.append(pltpu.make_async_copy(source, acts.at[e, place], sems.at[e, k]))
        return made

    @pl.when(example == 0)
    def _():
        for copy in copies(0) + copies(1):
            copy.start()
        for copy in copies(0):
            copy.wait()

    @pl.when(example == 1)
    def _():
        for copy in copies(1):
            copy.wait()

    columns = grads.shape[1]
    squares = jnp.zeros((1, LANES), jnp.float32)
    at = row = 0
    for h, (_, width) in enumerate(RAW):
        together = LANES // width
        rows = columns // together
        for tile in range(coded_ref.shape[0] // together):
            if at % CHUNK == 0:
                some = acts[example, :, at : at + CHUNK]
                product = jnp.dot(grads[example], some, preferred_element_type=jnp.float32)
                squares = squares + lane_sums(product)
            values = product[:, at % CHUNK : at % CHUNK + LANES]
            units, exponent = coded(values, tops(values))
            exponents = packed_row(exponent, together)
            for k, block in enumerate(packed(units, together)):
                coded_ref[tile * together + k, 0, row : row + rows] = narrow(block)
                exponent_ref[tile * together + k, 0, h : h + 1] = exponents[k]
            at += LANES
        row += rows
    squares_ref[0] = squares


def raw_products(order, pieces, grads):
    examples, shard, features = pieces[0].shape
    _, columns, positions = grads.shape
    owners = features // sum(width for _, width in RAW)
    rows = columns * features // owners // LANES
    return pl.pallas_call(
        raw_kernel,
        grid=(examples,),
        in_specs=[pl.BlockSpec(memory_space=pltpu.SMEM)]
        + [pl.BlockSpec(memory_space=pltpu.HBM)] * (len(pieces) + 1),
        out_specs=[
            pl.BlockSpec((owners, 1, rows, LANES), lambda e: (0, e, 0, 0)),
            pl.BlockSpec((owners, 1, 8, LANES), lambda e: (0, e, 0, 0)),
            pl.BlockSpec((1, 1, LANES), lambda e: (e, 0, 0)),
        ],
        out_shape=[
            jax.ShapeDtypeStruct((owners, examples, rows, LANES), jnp.int16),
            jax.ShapeDtypeStruct((owners, examples, 8, LANES), jnp.float32),
            jax.ShapeDtypeStruct((examples, 1, LANES), jnp.float32),
        ],
        scratch_shapes=[
            pltpu.VMEM((examples, positions, features), pieces[0].dtype),
            pltpu.VMEM(grads.shape, grads.dtype),
            pltpu.SemaphoreType.DMA((examples, len(order) + 1)),
        ],
        compiler_params=PARAMS,
    )(order, *pieces, grads)


def plain_kernel(acts_ref, grads_ref, squares_ref, product_ref, top_ref, share_ref, acts, grads, acts_sems, grads_sems):
    devices, examples, shard, _ = acts_ref.shape
    width = product_ref.shape[2]
    tiles = acts_ref.shape[3] // width
    example, tile = pl.program_id(0), pl.program_id(1)

    def acts_copy(step):
        here = pl.ds(step % tiles * width, width)
        source = acts_ref.at[:, step // tiles, :, here]
        return pltpu.make_async_copy(source, acts.at[step % 2], acts_sems.at[step % 2])

    def grads_copy(e):
        return pltpu.make_async_copy(grads_ref.at[e], grads.at[e], grads_sems.at[e])

    for step in range(examples * tiles):

        @pl.when(example * tiles + tile == step)
        def _():
            if step == 0:
                acts_copy(0).start()
                for e in range(examples):
                    grads_copy(e).start()
            if step + 1 < examples * tiles:
                acts_copy(step + 1).start()
            acts_copy(step).wait()
            if step % tiles == 0:
                grads_copy(step // tiles).wait()

    @pl.when(tile == 0)
    def _():
        share_ref[...] = squares_ref[...]

    slot = (example * tiles + tile) % 2
    share = share_ref[0]
    for at in range(0, width, CHUNK):
        here = slice(at, at + CHUNK)
        some = acts[slot, :, :, here].reshape(devices * shard, CHUNK)
        product = jnp.dot(grads[example], some, preferred_element_type=jnp.float32)
        product_ref[0, :, here] = product
        top_ref[0, :, here] = tops(product)
        share = share + lane_sums(product)
    share_ref[0] = share


def plain_products(acts, grads, squares):
    devices, examples, shard, features = acts.shape
    _, columns, _ = grads.shape
    width = features // 2
    row = pl.BlockSpec((1, 1, LANES), lambda e, i: (e, 0, 0))
    hbm = pl.BlockSpec(memory_space=pltpu.HBM)
    return pl.pallas_call(
        plain_kernel,
        grid=(examples, features // width),
        in_specs=[hbm, hbm, row],
        out_specs=[
            pl.BlockSpec((1, columns, width), lambda e, i: (e, 0, i)),
            pl.BlockSpec((1, 1, width), lambda e, i: (e, 0, i)),
            row,
        ],
        out_shape=[
            jax.ShapeDtypeStruct((examples, columns, features), jnp.float32),
            jax.ShapeDtypeStruct((examples, 1, features), jnp.float32),
            jax.ShapeDtypeStruct((examples, 1, LANES), jnp.float32),
        ],
        scratch_shapes=[
            pltpu.VMEM((2, devices, shard, width), acts.dtype),
            pltpu.VMEM(grads.shape, grads.dtype),
            pltpu.SemaphoreType.DMA((2,)),
            pltpu.SemaphoreType.DMA((examples,)),
        ],
        cost_estimate=SMALL,
        compiler_params=LESS,
    )(*(pltpu.with_memory_space_constraint(a, pltpu.HBM) for a in (acts, grads, squares)))


def clipped_kernel(clip_ref, shares_ref, wide_ref, thin_ref, wide_top_ref, thin_top_ref, exponent_ref, coded_ref):
    examples, columns, _ = wide_ref.shape
    owners = coded_ref.shape[0]
    clip = clip_ref[0]
    blank = jnp.zeros((1, LANES), jnp.float32)
    factors, extra = [], [[] for _ in range(owners)]
    for e in range(examples):
        square = jnp.sum(shares_ref[e], axis=1, keepdims=True)
        factor = clip / jnp.maximum(jnp.sqrt(square), clip)
        factors.append(factor)
        power = jnp.floor(jnp.log2(jnp.maximum(factor, LEAST))) + 1.0
        scaled = factor * jnp.exp2(-power) * 16384.0
        high = jnp.floor(scaled)
        low = jnp.round((scaled - high) * 16384.0)
        for k in range(owners):
            extra[k] += [blank + high, blank + low]
            extra[k] += [exponent_ref[k, e, h : h + 1] + power for h in range(len(RAW))]

    def added(ref, *at):
        return sum(factors[e] * ref[(e,) + at] for e in range(examples))

    everything = slice(None)
    thin_units, exponent = coded(added(thin_ref, everything, everything), added(thin_top_ref, everything, everything))
    thin_units, thin_exponents = packed(thin_units, owners), packed_row(exponent, owners)
    for k in range(owners):
        here = slice(k * LANES, (k + 1) * LANES)
        top = added(wide_top_ref, everything, here)
        for at in range(0, columns, LANES):
            rows = slice(at, at + LANES)
            units, exponent = coded(added(wide_ref, rows, here), top)
            coded_ref[k, rows] = narrow(units)
        rows = extra[k] + [exponent, thin_exponents[k]]
        rows = jnp.concatenate(rows + [blank] * (EXTRA - len(rows)), axis=0)
        coded_ref[k, columns : coded_ref.shape[1] - EXTRA] = narrow(thin_units[k])
        coded_ref[k, coded_ref.shape[1] - EXTRA :] = narrow(rows)


def clipped_sums(clip_bound, shares, products, top, exponents):
    examples, columns, features = products.shape
    owners = exponents.shape[0]
    together = LANES // CLIPPED[1][1]
    rows = columns * features // owners // LANES + EXTRA
    return pl.pallas_call(
        clipped_kernel,
        grid=(owners // together,),
        in_specs=[
            pl.BlockSpec(memory_space=pltpu.SMEM),
            pl.BlockSpec(shares.shape, lambda i: (0, 0, 0)),
            pl.BlockSpec((examples, columns, together * LANES), lambda i: (0, 0, i)),
            pl.BlockSpec((examples, columns, LANES), lambda i: (0, 0, owners + i)),
            pl.BlockSpec((examples, 1, together * LANES), lambda i: (0, 0, i)),
            pl.BlockSpec((examples, 1, LANES), lambda i: (0, 0, owners + i)),
            pl.BlockSpec((together, examples, 8, LANES), lambda i: (i, 0, 0, 0)),
        ],
        out_specs=pl.BlockSpec((together, rows, LANES), lambda i: (i, 0, 0)),
        out_shape=jax.ShapeDtypeStruct((owners, rows, LANES), jnp.int16),
        cost_estimate=SMALL,
        compiler_params=LESS,
    )(clip_bound, shares, products, products, top, top, exponents)


def finish_kernel(scale, raw_ref, clipped_ref, noise_ref, out_ref, raw_sum, clipped_sum):
    _, examples, _, _ = raw_ref.shape
    columns = out_ref.shape[1]
    group = pl.program_id(0)

    @pl.when(group == 0)
    def _():
        raw_sum[...] = jnp.zeros_like(raw_sum)
        clipped_sum[...] = jnp.zeros_like(clipped_sum)

    kinds = len(RAW)
    bottom = clipped_sum.shape[0]
    extra = [clipped_ref[g, bottom:].astype(jnp.float32) for g in range(TOGETHER)]
    row = lambda g, k: extra[g][k : k + 1]
    at = 0
    for h, (_, width) in enumerate(RAW):
        weights = []
        for g in range(TOGETHER):
            for e in range(examples):
                base = e * (2 + kinds)
                weight = (row(g, base) + row(g, base + 1) * (1.0 / 16384.0)) * (1.0 / 16384.0)
                weights.append((g, e, weight * jnp.exp2(row(g, base + 2 + h))))
        end = at + columns * width // LANES
        for block in range(at, end, LANES):
            rows = slice(block, block + LANES)
            raw_sum[rows] += sum(w * raw_ref[g, e, rows].astype(jnp.float32) for g, e, w in weights)
        at = end
    at = 0
    for h, (_, width) in enumerate(CLIPPED):
        steps = [jnp.exp2(row(g, examples * (2 + kinds) + h)) for g in range(TOGETHER)]
        end = at + columns * width // LANES
        for block in range(at, end, LANES):
            rows = slice(block, block + LANES)
            clipped_sum[rows] += sum(w * clipped_ref[g, rows].astype(jnp.float32) for g, w in enumerate(steps))
        at = end

    @pl.when(group == pl.num_programs(0) - 1)
    def _():
        for sums, parts in ((raw_sum, RAW), (clipped_sum, CLIPPED)):
            at = 0
            for first, width in parts:
                together = LANES // width
                rows = columns // together
                turned = sums[at : at + rows].T
                for k in range(together):
                    here = (slice(first, first + width), slice(k * rows, (k + 1) * rows))
                    out_ref[here] = turned[k * width : (k + 1) * width] * scale + noise_ref[here]
                at += rows


def finish(raw, clipped, noise, scale):
    groups, examples, raw_rows, _ = raw.shape
    rows = clipped.shape[1]
    whole = pl.BlockSpec(noise.shape, lambda g: (0, 0))
    return pl.pallas_call(
        functools.partial(finish_kernel, scale),
        grid=(groups // TOGETHER,),
        in_specs=[
            pl.BlockSpec((TOGETHER, examples, raw_rows, LANES), lambda g: (g, 0, 0, 0)),
            pl.BlockSpec((TOGETHER, rows, LANES), lambda g: (g, 0, 0)),
            whole,
        ],
        out_specs=whole,
        out_shape=jax.ShapeDtypeStruct(noise.shape, jnp.float32),
        scratch_shapes=[pltpu.VMEM((raw_rows, LANES), jnp.float32), pltpu.VMEM((rows - EXTRA, LANES), jnp.float32)],
        compiler_params=PARAMS,
    )(raw, clipped, noise)


def per_device(activations, out_grads, lengths, clip_bound, noise):
    owners = lax.axis_size("dp")
    devices = lax.axis_size("tensor")
    examples = activations.shape[0]
    here = lax.axis_index("tensor")

    def along_z(x, k):
        return lax.ppermute(x, "tensor", [(t, (t + 2 * k) % devices) for t in range(devices)])

    def crossed(x, k):
        return lax.ppermute(x, "tensor", [(t, t ^ k) for t in range(devices)])

    own = part_features(activations, RAW)
    positions = lax.broadcasted_iota(jnp.int32, (1, out_grads.shape[1], 1), 1)
    masked = jnp.where(positions < lengths[:, None, None], out_grads, jnp.zeros_like(out_grads))
    masked = jnp.swapaxes(masked, 1, 2)

    step = jnp.array([2 * k for k in ARRIVALS for _ in range(2)], jnp.int32)
    second_core = jnp.array([0, 1] * len(ARRIVALS), jnp.int32)
    order = ((here & ~1) + step + ((here & 1) ^ second_core)) & (devices - 1)

    up1, down1 = along_z(own, 1), along_z(own, -1)
    up1, down1, activations = lax.optimization_barrier((up1, down1, activations))
    up2, down2 = along_z(up1, 1), along_z(down1, -1)
    second = lax.all_gather(part_features(activations, CLIPPED), "tensor")
    up2, down2, masked, order = lax.optimization_barrier((up2, down2, masked, order))
    up3, down3 = along_z(up2, 1), along_z(down2, -1)
    up4, down4 = along_z(up3[:1], 1), along_z(down3[1:], -1)
    pieces = []
    for piece in (own, up1, down1, up2, down2, up3, down3):
        pieces += [piece, crossed(piece, 1)]
    pieces += [up4, crossed(up4, 1), down4, crossed(down4, 1)]

    raw, exponents, squares = raw_products(order, pieces, masked)
    raw = lax.all_to_all(raw, "dp", 0, 0)
    products, top, share = plain_products(second, masked, squares)
    share = share + crossed(share, 1) + crossed(share, 2) + crossed(share, 3)
    share = share + crossed(share, 4) + crossed(share, 8) + crossed(share, 12)
    clipped = clipped_sums(clip_bound, share, products, top, exponents)
    clipped, raw = lax.optimization_barrier((clipped, raw))
    clipped = lax.all_to_all(clipped, "dp", 0, 0)
    return finish(raw, clipped, noise, float((examples * owners) ** -0.5))


def solution(mesh):
    in_specs = (P("dp", "tensor", None), P("dp", None, "tensor"), P("dp"), P(), P("dp", "tensor"))
    out_specs = P("dp", "tensor")
    return jax.shard_map(
        per_device, mesh=mesh, in_specs=in_specs, out_specs=out_specs, check_vma=False
    )
```

```python
import functools

import jax
import jax.numpy as jnp
from jax import lax
from jax.experimental import pallas as pl
from jax.experimental.pallas import tpu as pltpu
from jax.sharding import PartitionSpec as P

LANES = 128
EXTRA = 16
TOGETHER = 8
LEAST = 1e-33
CHUNK = 256
PARAMS = pltpu.CompilerParams(vmem_limit_bytes=56 * 1024 * 1024)
LESS = pltpu.CompilerParams(vmem_limit_bytes=28 * 1024 * 1024)
RAW = ((0, 64), (64, 32))
CLIPPED = ((128, 128), (96, 32))
OWNED = sum(width for _, width in RAW + CLIPPED)
ARRIVALS = (0, -1, 1, -2, 2, -3, 3, 4)
SMALL = pl.CostEstimate(flops=1, bytes_accessed=1, transcendentals=0)


def part_kernel(parts, acts_ref, part_ref):
    at = 0
    for first, width in parts:
        for tile in range(acts_ref.shape[1] // OWNED * width // LANES):
            owners = range(tile * LANES // width, (tile + 1) * LANES // width)
            pieces = [acts_ref[:, o * OWNED + first : o * OWNED + first + width] for o in owners]
            part_ref[:, at : at + LANES] = jnp.concatenate(pieces, axis=1) if len(pieces) > 1 else pieces[0]
            at += LANES


def part_features(acts, parts):
    examples, shard, features = acts.shape
    taken = features // OWNED * sum(width for _, width in parts)
    return pl.pallas_call(
        functools.partial(part_kernel, parts),
        grid=(examples,),
        in_specs=[pl.BlockSpec((shard, features), lambda e: (e, 0))],
        out_specs=pl.BlockSpec((shard, taken), lambda e: (e, 0)),
        out_shape=jax.ShapeDtypeStruct((examples * shard, taken), acts.dtype),
        compiler_params=PARAMS,
    )(acts.reshape(examples * shard, features)).reshape(examples, shard, taken)


def tops(values):
    return jnp.max(jnp.abs(values), axis=0, keepdims=True)


def coded(values, top):
    exponent = jnp.ceil(jnp.log2(jnp.maximum(top, LEAST)) - 14.99)
    return jnp.round(values * jnp.exp2(-exponent)), exponent


def narrow(units):
    return units.astype(jnp.int32).astype(jnp.int16)


def packed(tile, owners):
    if owners == 1:
        return [tile]
    width, rows = LANES // owners, tile.shape[0] // owners
    lane = lax.broadcasted_iota(jnp.int32, (rows, LANES), 1)
    out = []
    for owner in range(owners):
        total = None
        for group in range(owners):
            piece = tile[group * rows : (group + 1) * rows]
            shift = (group - owner) * width % LANES
            piece = pltpu.roll(piece, shift, 1) if shift else piece
            total = piece if total is None else jnp.where(lane >= group * width, piece, total)
        out.append(total)
    return out


def packed_row(row, owners):
    return [t[0:1] for t in packed(jnp.broadcast_to(row, (8 * owners, LANES)), owners)]


def lane_sums(product):
    rows = jnp.sum(product * product, axis=0, keepdims=True)
    return sum(rows[:, at : at + LANES] for at in range(0, rows.shape[1], LANES))


def raw_kernel(order_ref, *refs):
    pieces, (grads_ref, coded_ref, exponent_ref, squares_ref, acts, grads, sems) = refs[:-7], refs[-7:]
    example = pl.program_id(0)
    depth = pieces[0].shape[1]

    def copies(e):
        far = pieces[-4 + 2 * e : len(pieces) - 2 + 2 * e]
        sources = [p.at[e] for p in pieces[:-4]] + [p.at[0] for p in far]
        made = [pltpu.make_async_copy(grads_ref.at[e], grads.at[e], sems.at[e, len(sources)])]
        for k, source in enumerate(sources):
            place = pl.ds(pl.multiple_of(order_ref[k] * depth, depth), depth)
            made.append(pltpu.make_async_copy(source, acts.at[e, place], sems.at[e, k]))
        return made

    @pl.when(example == 0)
    def _():
        for copy in copies(0) + copies(1):
            copy.start()
        for copy in copies(0):
            copy.wait()

    @pl.when(example == 1)
    def _():
        for copy in copies(1):
            copy.wait()

    columns = grads.shape[1]
    squares = jnp.zeros((1, LANES), jnp.float32)
    at = row = 0
    for h, (_, width) in enumerate(RAW):
        together = LANES // width
        rows = columns // together
        for tile in range(coded_ref.shape[0] // together):
            if at % CHUNK == 0:
                some = acts[example, :, at : at + CHUNK]
                product = jnp.dot(grads[example], some, preferred_element_type=jnp.float32)
                squares = squares + lane_sums(product)
            values = product[:, at % CHUNK : at % CHUNK + LANES]
            units, exponent = coded(values, tops(values))
            exponents = packed_row(exponent, together)
            for k, block in enumerate(packed(units, together)):
                coded_ref[tile * together + k, 0, row : row + rows] = narrow(block)
                exponent_ref[tile * together + k, 0, h : h + 1] = exponents[k]
            at += LANES
        row += rows
    squares_ref[0] = squares


def raw_products(order, pieces, grads):
    examples, shard, features = pieces[0].shape
    _, columns, positions = grads.shape
    owners = features // sum(width for _, width in RAW)
    rows = columns * features // owners // LANES
    return pl.pallas_call(
        raw_kernel,
        grid=(examples,),
        in_specs=[pl.BlockSpec(memory_space=pltpu.SMEM)]
        + [pl.BlockSpec(memory_space=pltpu.HBM)] * (len(pieces) + 1),
        out_specs=[
            pl.BlockSpec((owners, 1, rows, LANES), lambda e: (0, e, 0, 0)),
            pl.BlockSpec((owners, 1, 8, LANES), lambda e: (0, e, 0, 0)),
            pl.BlockSpec((1, 1, LANES), lambda e: (e, 0, 0)),
        ],
        out_shape=[
            jax.ShapeDtypeStruct((owners, examples, rows, LANES), jnp.int16),
            jax.ShapeDtypeStruct((owners, examples, 8, LANES), jnp.float32),
            jax.ShapeDtypeStruct((examples, 1, LANES), jnp.float32),
        ],
        scratch_shapes=[
            pltpu.VMEM((examples, positions, features), pieces[0].dtype),
            pltpu.VMEM(grads.shape, grads.dtype),
            pltpu.SemaphoreType.DMA((examples, len(order) + 1)),
        ],
        compiler_params=PARAMS,
    )(order, *pieces, grads)


def plain_kernel(acts_ref, grads_ref, squares_ref, product_ref, top_ref, share_ref, acts, grads, acts_sems, grads_sems):
    devices, examples, shard, _ = acts_ref.shape
    width = product_ref.shape[2]
    tiles = acts_ref.shape[3] // width
    example, tile = pl.program_id(0), pl.program_id(1)

    def acts_copy(step):
        here = pl.ds(step % tiles * width, width)
        source = acts_ref.at[:, step // tiles, :, here]
        return pltpu.make_async_copy(source, acts.at[step % 2], acts_sems.at[step % 2])

    def grads_copy(e):
        return pltpu.make_async_copy(grads_ref.at[e], grads.at[e], grads_sems.at[e])

    for step in range(examples * tiles):

        @pl.when(example * tiles + tile == step)
        def _():
            if step == 0:
                acts_copy(0).start()
                for e in range(examples):
                    grads_copy(e).start()
            if step + 1 < examples * tiles:
                acts_copy(step + 1).start()
            acts_copy(step).wait()
            if step % tiles == 0:
                grads_copy(step // tiles).wait()

    @pl.when(tile == 0)
    def _():
        share_ref[...] = squares_ref[...]

    slot = (example * tiles + tile) % 2
    share = share_ref[0]
    for at in range(0, width, CHUNK):
        here = slice(at, at + CHUNK)
        some = acts[slot, :, :, here].reshape(devices * shard, CHUNK)
        product = jnp.dot(grads[example], some, preferred_element_type=jnp.float32)
        product_ref[0, :, here] = product
        top_ref[0, :, here] = tops(product)
        share = share + lane_sums(product)
    share_ref[0] = share


def plain_products(acts, grads, squares):
    devices, examples, shard, features = acts.shape
    _, columns, _ = grads.shape
    width = features // 2
    row = pl.BlockSpec((1, 1, LANES), lambda e, i: (e, 0, 0))
    hbm = pl.BlockSpec(memory_space=pltpu.HBM)
    return pl.pallas_call(
        plain_kernel,
        grid=(examples, features // width),
        in_specs=[hbm, hbm, row],
        out_specs=[
            pl.BlockSpec((1, columns, width), lambda e, i: (e, 0, i)),
            pl.BlockSpec((1, 1, width), lambda e, i: (e, 0, i)),
            row,
        ],
        out_shape=[
            jax.ShapeDtypeStruct((examples, columns, features), jnp.float32),
            jax.ShapeDtypeStruct((examples, 1, features), jnp.float32),
            jax.ShapeDtypeStruct((examples, 1, LANES), jnp.float32),
        ],
        scratch_shapes=[
            pltpu.VMEM((2, devices, shard, width), acts.dtype),
            pltpu.VMEM(grads.shape, grads.dtype),
            pltpu.SemaphoreType.DMA((2,)),
            pltpu.SemaphoreType.DMA((examples,)),
        ],
        cost_estimate=SMALL,
        compiler_params=LESS,
    )(*(pltpu.with_memory_space_constraint(a, pltpu.HBM) for a in (acts, grads, squares)))


def clipped_kernel(clip_ref, shares_ref, wide_ref, thin_ref, wide_top_ref, thin_top_ref, exponent_ref, coded_ref):
    examples, columns, _ = wide_ref.shape
    owners = coded_ref.shape[0]
    clip = clip_ref[0]
    blank = jnp.zeros((1, LANES), jnp.float32)
    factors, extra = [], [[] for _ in range(owners)]
    for e in range(examples):
        square = jnp.sum(shares_ref[e], axis=1, keepdims=True)
        factor = clip / jnp.maximum(jnp.sqrt(square), clip)
        factors.append(factor)
        power = jnp.floor(jnp.log2(jnp.maximum(factor, LEAST))) + 1.0
        scaled = factor * jnp.exp2(-power) * 16384.0
        high = jnp.floor(scaled)
        low = jnp.round((scaled - high) * 16384.0)
        for k in range(owners):
            extra[k] += [blank + high, blank + low]
            extra[k] += [exponent_ref[k, e, h : h + 1] + power for h in range(len(RAW))]

    def added(ref, *at):
        return sum(factors[e] * ref[(e,) + at] for e in range(examples))

    everything = slice(None)
    thin_units, exponent = coded(added(thin_ref, everything, everything), added(thin_top_ref, everything, everything))
    thin_units, thin_exponents = packed(thin_units, owners), packed_row(exponent, owners)
    for k in range(owners):
        here = slice(k * LANES, (k + 1) * LANES)
        top = added(wide_top_ref, everything, here)
        for at in range(0, columns, LANES):
            rows = slice(at, at + LANES)
            units, exponent = coded(added(wide_ref, rows, here), top)
            coded_ref[k, rows] = narrow(units)
        rows = extra[k] + [exponent, thin_exponents[k]]
        rows = jnp.concatenate(rows + [blank] * (EXTRA - len(rows)), axis=0)
        coded_ref[k, columns : coded_ref.shape[1] - EXTRA] = narrow(thin_units[k])
        coded_ref[k, coded_ref.shape[1] - EXTRA :] = narrow(rows)


def clipped_sums(clip_bound, shares, products, top, exponents):
    examples, columns, features = products.shape
    owners = exponents.shape[0]
    together = LANES // CLIPPED[1][1]
    rows = columns * features // owners // LANES + EXTRA
    return pl.pallas_call(
        clipped_kernel,
        grid=(owners // together,),
        in_specs=[
            pl.BlockSpec(memory_space=pltpu.SMEM),
            pl.BlockSpec(shares.shape, lambda i: (0, 0, 0)),
            pl.BlockSpec((examples, columns, together * LANES), lambda i: (0, 0, i)),
            pl.BlockSpec((examples, columns, LANES), lambda i: (0, 0, owners + i)),
            pl.BlockSpec((examples, 1, together * LANES), lambda i: (0, 0, i)),
            pl.BlockSpec((examples, 1, LANES), lambda i: (0, 0, owners + i)),
            pl.BlockSpec((together, examples, 8, LANES), lambda i: (i, 0, 0, 0)),
        ],
        out_specs=pl.BlockSpec((together, rows, LANES), lambda i: (i, 0, 0)),
        out_shape=jax.ShapeDtypeStruct((owners, rows, LANES), jnp.int16),
        cost_estimate=SMALL,
        compiler_params=LESS,
    )(clip_bound, shares, products, products, top, top, exponents)


def finish_kernel(scale, raw_ref, clipped_ref, noise_ref, out_ref, raw_sum, clipped_sum):
    _, examples, _, _ = raw_ref.shape
    columns = out_ref.shape[1]
    group = pl.program_id(0)

    @pl.when(group == 0)
    def _():
        raw_sum[...] = jnp.zeros_like(raw_sum)
        clipped_sum[...] = jnp.zeros_like(clipped_sum)

    kinds = len(RAW)
    bottom = clipped_sum.shape[0]
    extra = [clipped_ref[g, bottom:].astype(jnp.float32) for g in range(TOGETHER)]
    row = lambda g, k: extra[g][k : k + 1]
    at = 0
    for h, (_, width) in enumerate(RAW):
        weights = []
        for g in range(TOGETHER):
            for e in range(examples):
                base = e * (2 + kinds)
                weight = (row(g, base) + row(g, base + 1) * (1.0 / 16384.0)) * (1.0 / 16384.0)
                weights.append((g, e, weight * jnp.exp2(row(g, base + 2 + h))))
        end = at + columns * width // LANES
        for block in range(at, end, LANES):
            rows = slice(block, block + LANES)
            raw_sum[rows] += sum(w * raw_ref[g, e, rows].astype(jnp.float32) for g, e, w in weights)
        at = end
    at = 0
    for h, (_, width) in enumerate(CLIPPED):
        steps = [jnp.exp2(row(g, examples * (2 + kinds) + h)) for g in range(TOGETHER)]
        end = at + columns * width // LANES
        for block in range(at, end, LANES):
            rows = slice(block, block + LANES)
            clipped_sum[rows] += sum(w * clipped_ref[g, rows].astype(jnp.float32) for g, w in enumerate(steps))
        at = end

    @pl.when(group == pl.num_programs(0) - 1)
    def _():
        for sums, parts in ((raw_sum, RAW), (clipped_sum, CLIPPED)):
            at = 0
            for first, width in parts:
                together = LANES // width
                rows = columns // together
                turned = sums[at : at + rows].T
                for k in range(together):
                    here = (slice(first, first + width), slice(k * rows, (k + 1) * rows))
                    out_ref[here] = turned[k * width : (k + 1) * width] * scale + noise_ref[here]
                at += rows


def finish(raw, clipped, noise, scale):
    groups, examples, raw_rows, _ = raw.shape
    rows = clipped.shape[1]
    whole = pl.BlockSpec(noise.shape, lambda g: (0, 0))
    return pl.pallas_call(
        functools.partial(finish_kernel, scale),
        grid=(groups // TOGETHER,),
        in_specs=[
            pl.BlockSpec((TOGETHER, examples, raw_rows, LANES), lambda g: (g, 0, 0, 0)),
            pl.BlockSpec((TOGETHER, rows, LANES), lambda g: (g, 0, 0)),
            whole,
        ],
        out_specs=whole,
        out_shape=jax.ShapeDtypeStruct(noise.shape, jnp.float32),
        scratch_shapes=[pltpu.VMEM((raw_rows, LANES), jnp.float32), pltpu.VMEM((rows - EXTRA, LANES), jnp.float32)],
        compiler_params=PARAMS,
    )(raw, clipped, noise)


def per_device(activations, out_grads, lengths, clip_bound, noise):
    owners = lax.axis_size("dp")
    devices = lax.axis_size("tensor")
    examples = activations.shape[0]
    here = lax.axis_index("tensor")

    def along_z(x, k):
        return lax.ppermute(x, "tensor", [(t, (t + 2 * k) % devices) for t in range(devices)])

    def crossed(x, k):
        return lax.ppermute(x, "tensor", [(t, t ^ k) for t in range(devices)])

    own = part_features(activations, RAW)
    second = part_features(activations, CLIPPED)
    positions = lax.broadcasted_iota(jnp.int32, (1, out_grads.shape[1], 1), 1)
    masked = jnp.where(positions < lengths[:, None, None], out_grads, jnp.zeros_like(out_grads))
    masked = jnp.swapaxes(masked, 1, 2)

    step = jnp.array([2 * k for k in ARRIVALS for _ in range(2)], jnp.int32)
    second_core = jnp.array([0, 1] * len(ARRIVALS), jnp.int32)
    order = ((here & ~1) + step + ((here & 1) ^ second_core)) & (devices - 1)

    up1, down1 = along_z(own, 1), along_z(own, -1)
    up2, down2 = along_z(up1, 1), along_z(down1, -1)
    up2, down2, second, masked, order = lax.optimization_barrier((up2, down2, second, masked, order))
    second = lax.all_gather(second, "tensor")
    up3, down3 = along_z(up2, 1), along_z(down2, -1)
    up4, down4 = along_z(up3[:1], 1), along_z(down3[1:], -1)
    pieces = []
    for piece in (own, up1, down1, up2, down2, up3, down3):
        pieces += [piece, crossed(piece, 1)]
    pieces += [up4, crossed(up4, 1), down4, crossed(down4, 1)]

    raw, exponents, squares = raw_products(order, pieces, masked)
    raw = lax.all_to_all(raw, "dp", 0, 0)
    products, top, share = plain_products(second, masked, squares)
    share = share + crossed(share, 1) + crossed(share, 2) + crossed(share, 3)
    share = share + crossed(share, 4) + crossed(share, 8) + crossed(share, 12)
    clipped = clipped_sums(clip_bound, share, products, top, exponents)
    clipped, raw = lax.optimization_barrier((clipped, raw))
    clipped = lax.all_to_all(clipped, "dp", 0, 0)
    return finish(raw, clipped, noise, float((examples * owners) ** -0.5))


def solution(mesh):
    in_specs = (P("dp", "tensor", None), P("dp", None, "tensor"), P("dp"), P(), P("dp", "tensor"))
    out_specs = P("dp", "tensor")
    return jax.shard_map(
        per_device, mesh=mesh, in_specs=in_specs, out_specs=out_specs, check_vma=False
    )
```

```python
import functools

import jax
import jax.numpy as jnp
from jax import lax
from jax.experimental import pallas as pl
from jax.experimental.pallas import tpu as pltpu
from jax.sharding import PartitionSpec as P

LANES = 128
EXTRA = 16
TOGETHER = 8
LEAST = 1e-33
CHUNK = 256
WIDER = 640
PARAMS = pltpu.CompilerParams(vmem_limit_bytes=56 * 1024 * 1024)
LESS = pltpu.CompilerParams(vmem_limit_bytes=28 * 1024 * 1024)
RAW = ((0, 64), (64, 32))
CLIPPED = ((128, 128), (96, 32))
OWNED = sum(width for _, width in RAW + CLIPPED)
ARRIVALS = (0, -1, 1, -2, 2, -3, 3, 4)
SMALL = pl.CostEstimate(flops=1, bytes_accessed=1, transcendentals=0)


def part_kernel(parts, acts_ref, part_ref):
    at = 0
    for first, width in parts:
        for tile in range(acts_ref.shape[1] // OWNED * width // LANES):
            owners = range(tile * LANES // width, (tile + 1) * LANES // width)
            pieces = [acts_ref[:, o * OWNED + first : o * OWNED + first + width] for o in owners]
            part_ref[:, at : at + LANES] = jnp.concatenate(pieces, axis=1) if len(pieces) > 1 else pieces[0]
            at += LANES


def part_features(acts, parts):
    examples, shard, features = acts.shape
    taken = features // OWNED * sum(width for _, width in parts)
    return pl.pallas_call(
        functools.partial(part_kernel, parts),
        grid=(examples,),
        in_specs=[pl.BlockSpec((shard, features), lambda e: (e, 0))],
        out_specs=pl.BlockSpec((shard, taken), lambda e: (e, 0)),
        out_shape=jax.ShapeDtypeStruct((examples * shard, taken), acts.dtype),
        compiler_params=PARAMS,
    )(acts.reshape(examples * shard, features)).reshape(examples, shard, taken)


def tops(values):
    return jnp.max(jnp.abs(values), axis=0, keepdims=True)


def coded(values, top):
    exponent = jnp.ceil(jnp.log2(jnp.maximum(top, LEAST)) - 14.99)
    return jnp.round(values * jnp.exp2(-exponent)), exponent


def narrow(units):
    return units.astype(jnp.int32).astype(jnp.int16)


def packed(tile, owners):
    if owners == 1:
        return [tile]
    width, rows = LANES // owners, tile.shape[0] // owners
    lane = lax.broadcasted_iota(jnp.int32, (rows, LANES), 1)
    out = []
    for owner in range(owners):
        total = None
        for group in range(owners):
            piece = tile[group * rows : (group + 1) * rows]
            shift = (group - owner) * width % LANES
            piece = pltpu.roll(piece, shift, 1) if shift else piece
            total = piece if total is None else jnp.where(lane >= group * width, piece, total)
        out.append(total)
    return out


def packed_row(row, owners):
    return [t[0:1] for t in packed(jnp.broadcast_to(row, (8 * owners, LANES)), owners)]


def lane_sums(product):
    rows = jnp.sum(product * product, axis=0, keepdims=True)
    return sum(rows[:, at : at + LANES] for at in range(0, rows.shape[1], LANES))


def raw_kernel(order_ref, *refs):
    pieces, (grads_ref, coded_ref, exponent_ref, squares_ref, acts, grads, sems) = refs[:-7], refs[-7:]
    example = pl.program_id(0)
    depth = pieces[0].shape[1]

    def copies(e):
        far = pieces[-4 + 2 * e : len(pieces) - 2 + 2 * e]
        sources = [p.at[e] for p in pieces[:-4]] + [p.at[0] for p in far]
        made = [pltpu.make_async_copy(grads_ref.at[e], grads.at[e], sems.at[e, len(sources)])]
        for k, source in enumerate(sources):
            place = pl.ds(pl.multiple_of(order_ref[k] * depth, depth), depth)
            made.append(pltpu.make_async_copy(source, acts.at[e, place], sems.at[e, k]))
        return made

    @pl.when(example == 0)
    def _():
        for copy in copies(0) + copies(1):
            copy.start()
        for copy in copies(0):
            copy.wait()

    @pl.when(example == 1)
    def _():
        for copy in copies(1):
            copy.wait()

    columns = grads.shape[1]
    squares = jnp.zeros((1, LANES), jnp.float32)
    at = row = 0
    for h, (_, width) in enumerate(RAW):
        together = LANES // width
        rows = columns // together
        for tile in range(coded_ref.shape[0] // together):
            if at % CHUNK == 0:
                some = acts[example, :, at : at + CHUNK]
                product = jnp.dot(grads[example], some, preferred_element_type=jnp.float32)
                squares = squares + lane_sums(product)
            values = product[:, at % CHUNK : at % CHUNK + LANES]
            units, exponent = coded(values, tops(values))
            exponents = packed_row(exponent, together)
            for k, block in enumerate(packed(units, together)):
                coded_ref[tile * together + k, 0, row : row + rows] = narrow(block)
                exponent_ref[tile * together + k, 0, h : h + 1] = exponents[k]
            at += LANES
        row += rows
    squares_ref[0] = squares


def raw_products(order, pieces, grads):
    examples, shard, features = pieces[0].shape
    _, columns, positions = grads.shape
    owners = features // sum(width for _, width in RAW)
    rows = columns * features // owners // LANES
    return pl.pallas_call(
        raw_kernel,
        grid=(examples,),
        in_specs=[pl.BlockSpec(memory_space=pltpu.SMEM)]
        + [pl.BlockSpec(memory_space=pltpu.HBM)] * (len(pieces) + 1),
        out_specs=[
            pl.BlockSpec((owners, 1, rows, LANES), lambda e: (0, e, 0, 0)),
            pl.BlockSpec((owners, 1, 8, LANES), lambda e: (0, e, 0, 0)),
            pl.BlockSpec((1, 1, LANES), lambda e: (e, 0, 0)),
        ],
        out_shape=[
            jax.ShapeDtypeStruct((owners, examples, rows, LANES), jnp.int16),
            jax.ShapeDtypeStruct((owners, examples, 8, LANES), jnp.float32),
            jax.ShapeDtypeStruct((examples, 1, LANES), jnp.float32),
        ],
        scratch_shapes=[
            pltpu.VMEM((examples, positions, features), pieces[0].dtype),
            pltpu.VMEM(grads.shape, grads.dtype),
            pltpu.SemaphoreType.DMA((examples, len(order) + 1)),
        ],
        compiler_params=PARAMS,
    )(order, *pieces, grads)


def plain_kernel(acts_ref, grads_ref, squares_ref, product_ref, top_ref, share_ref, acts, grads, acts_sems, grads_sems):
    devices, examples, shard, _ = acts_ref.shape
    width = product_ref.shape[2]
    tiles = acts_ref.shape[3] // width
    example, tile = pl.program_id(0), pl.program_id(1)

    def acts_copy(step):
        here = pl.ds(step % tiles * width, width)
        source = acts_ref.at[:, step // tiles, :, here]
        return pltpu.make_async_copy(source, acts.at[step % 2], acts_sems.at[step % 2])

    def grads_copy(e):
        return pltpu.make_async_copy(grads_ref.at[e], grads.at[e], grads_sems.at[e])

    for step in range(examples * tiles):

        @pl.when(example * tiles + tile == step)
        def _():
            if step == 0:
                acts_copy(0).start()
                for e in range(examples):
                    grads_copy(e).start()
            if step + 1 < examples * tiles:
                acts_copy(step + 1).start()
            acts_copy(step).wait()
            if step % tiles == 0:
                grads_copy(step // tiles).wait()

    @pl.when(tile == 0)
    def _():
        share_ref[...] = squares_ref[...]

    slot = (example * tiles + tile) % 2
    share = share_ref[0]
    for at in range(0, width, WIDER):
        here = slice(at, at + WIDER)
        some = acts[slot, :, :, here].reshape(devices * shard, WIDER)
        product = jnp.dot(grads[example], some, preferred_element_type=jnp.float32)
        product_ref[0, :, here] = product
        top_ref[0, :, here] = tops(product)
        share = share + lane_sums(product)
    share_ref[0] = share


def plain_products(acts, grads, squares):
    devices, examples, shard, features = acts.shape
    _, columns, _ = grads.shape
    width = features // 2
    row = pl.BlockSpec((1, 1, LANES), lambda e, i: (e, 0, 0))
    hbm = pl.BlockSpec(memory_space=pltpu.HBM)
    return pl.pallas_call(
        plain_kernel,
        grid=(examples, features // width),
        in_specs=[hbm, hbm, row],
        out_specs=[
            pl.BlockSpec((1, columns, width), lambda e, i: (e, 0, i)),
            pl.BlockSpec((1, 1, width), lambda e, i: (e, 0, i)),
            row,
        ],
        out_shape=[
            jax.ShapeDtypeStruct((examples, columns, features), jnp.float32),
            jax.ShapeDtypeStruct((examples, 1, features), jnp.float32),
            jax.ShapeDtypeStruct((examples, 1, LANES), jnp.float32),
        ],
        scratch_shapes=[
            pltpu.VMEM((2, devices, shard, width), acts.dtype),
            pltpu.VMEM(grads.shape, grads.dtype),
            pltpu.SemaphoreType.DMA((2,)),
            pltpu.SemaphoreType.DMA((examples,)),
        ],
        cost_estimate=SMALL,
        compiler_params=LESS,
    )(*(pltpu.with_memory_space_constraint(a, pltpu.HBM) for a in (acts, grads, squares)))


def clipped_kernel(clip_ref, shares_ref, wide_ref, thin_ref, wide_top_ref, thin_top_ref, exponent_ref, coded_ref):
    examples, columns, _ = wide_ref.shape
    owners = coded_ref.shape[0]
    clip = clip_ref[0]
    blank = jnp.zeros((1, LANES), jnp.float32)
    factors, extra = [], [[] for _ in range(owners)]
    for e in range(examples):
        square = jnp.sum(shares_ref[e], axis=1, keepdims=True)
        factor = clip / jnp.maximum(jnp.sqrt(square), clip)
        factors.append(factor)
        power = jnp.floor(jnp.log2(jnp.maximum(factor, LEAST))) + 1.0
        scaled = factor * jnp.exp2(-power) * 16384.0
        high = jnp.floor(scaled)
        low = jnp.round((scaled - high) * 16384.0)
        for k in range(owners):
            extra[k] += [blank + high, blank + low]
            extra[k] += [exponent_ref[k, e, h : h + 1] + power for h in range(len(RAW))]

    def added(ref, *at):
        return sum(factors[e] * ref[(e,) + at] for e in range(examples))

    everything = slice(None)
    thin_units, exponent = coded(added(thin_ref, everything, everything), added(thin_top_ref, everything, everything))
    thin_units, thin_exponents = packed(thin_units, owners), packed_row(exponent, owners)
    for k in range(owners):
        here = slice(k * LANES, (k + 1) * LANES)
        top = added(wide_top_ref, everything, here)
        for at in range(0, columns, LANES):
            rows = slice(at, at + LANES)
            units, exponent = coded(added(wide_ref, rows, here), top)
            coded_ref[k, rows] = narrow(units)
        rows = extra[k] + [exponent, thin_exponents[k]]
        rows = jnp.concatenate(rows + [blank] * (EXTRA - len(rows)), axis=0)
        coded_ref[k, columns : coded_ref.shape[1] - EXTRA] = narrow(thin_units[k])
        coded_ref[k, coded_ref.shape[1] - EXTRA :] = narrow(rows)


def clipped_sums(clip_bound, shares, products, top, exponents):
    examples, columns, features = products.shape
    owners = exponents.shape[0]
    together = LANES // CLIPPED[1][1]
    rows = columns * features // owners // LANES + EXTRA
    return pl.pallas_call(
        clipped_kernel,
        grid=(owners // together,),
        in_specs=[
            pl.BlockSpec(memory_space=pltpu.SMEM),
            pl.BlockSpec(shares.shape, lambda i: (0, 0, 0)),
            pl.BlockSpec((examples, columns, together * LANES), lambda i: (0, 0, i)),
            pl.BlockSpec((examples, columns, LANES), lambda i: (0, 0, owners + i)),
            pl.BlockSpec((examples, 1, together * LANES), lambda i: (0, 0, i)),
            pl.BlockSpec((examples, 1, LANES), lambda i: (0, 0, owners + i)),
            pl.BlockSpec((together, examples, 8, LANES), lambda i: (i, 0, 0, 0)),
        ],
        out_specs=pl.BlockSpec((together, rows, LANES), lambda i: (i, 0, 0)),
        out_shape=jax.ShapeDtypeStruct((owners, rows, LANES), jnp.int16),
        cost_estimate=SMALL,
        compiler_params=LESS,
    )(clip_bound, shares, products, products, top, top, exponents)


def finish_kernel(scale, raw_ref, clipped_ref, noise_ref, out_ref, raw_sum, clipped_sum):
    _, examples, _, _ = raw_ref.shape
    columns = out_ref.shape[1]
    group = pl.program_id(0)

    @pl.when(group == 0)
    def _():
        raw_sum[...] = jnp.zeros_like(raw_sum)
        clipped_sum[...] = jnp.zeros_like(clipped_sum)

    kinds = len(RAW)
    bottom = clipped_sum.shape[0]
    extra = [clipped_ref[g, bottom:].astype(jnp.float32) for g in range(TOGETHER)]
    row = lambda g, k: extra[g][k : k + 1]
    at = 0
    for h, (_, width) in enumerate(RAW):
        weights = []
        for g in range(TOGETHER):
            for e in range(examples):
                base = e * (2 + kinds)
                weight = (row(g, base) + row(g, base + 1) * (1.0 / 16384.0)) * (1.0 / 16384.0)
                weights.append((g, e, weight * jnp.exp2(row(g, base + 2 + h))))
        end = at + columns * width // LANES
        for block in range(at, end, LANES):
            rows = slice(block, block + LANES)
            raw_sum[rows] += sum(w * raw_ref[g, e, rows].astype(jnp.float32) for g, e, w in weights)
        at = end
    at = 0
    for h, (_, width) in enumerate(CLIPPED):
        steps = [jnp.exp2(row(g, examples * (2 + kinds) + h)) for g in range(TOGETHER)]
        end = at + columns * width // LANES
        for block in range(at, end, LANES):
            rows = slice(block, block + LANES)
            clipped_sum[rows] += sum(w * clipped_ref[g, rows].astype(jnp.float32) for g, w in enumerate(steps))
        at = end

    @pl.when(group == pl.num_programs(0) - 1)
    def _():
        for sums, parts in ((raw_sum, RAW), (clipped_sum, CLIPPED)):
            at = 0
            for first, width in parts:
                together = LANES // width
                rows = columns // together
                turned = sums[at : at + rows].T
                for k in range(together):
                    here = (slice(first, first + width), slice(k * rows, (k + 1) * rows))
                    out_ref[here] = turned[k * width : (k + 1) * width] * scale + noise_ref[here]
                at += rows


def finish(raw, clipped, noise, scale):
    groups, examples, raw_rows, _ = raw.shape
    rows = clipped.shape[1]
    whole = pl.BlockSpec(noise.shape, lambda g: (0, 0))
    return pl.pallas_call(
        functools.partial(finish_kernel, scale),
        grid=(groups // TOGETHER,),
        in_specs=[
            pl.BlockSpec((TOGETHER, examples, raw_rows, LANES), lambda g: (g, 0, 0, 0)),
            pl.BlockSpec((TOGETHER, rows, LANES), lambda g: (g, 0, 0)),
            whole,
        ],
        out_specs=whole,
        out_shape=jax.ShapeDtypeStruct(noise.shape, jnp.float32),
        scratch_shapes=[pltpu.VMEM((raw_rows, LANES), jnp.float32), pltpu.VMEM((rows - EXTRA, LANES), jnp.float32)],
        compiler_params=PARAMS,
    )(raw, clipped, noise)


def per_device(activations, out_grads, lengths, clip_bound, noise):
    owners = lax.axis_size("dp")
    devices = lax.axis_size("tensor")
    examples = activations.shape[0]
    here = lax.axis_index("tensor")

    def along_z(x, k):
        return lax.ppermute(x, "tensor", [(t, (t + 2 * k) % devices) for t in range(devices)])

    def crossed(x, k):
        return lax.ppermute(x, "tensor", [(t, t ^ k) for t in range(devices)])

    own = part_features(activations, RAW)
    second = part_features(activations, CLIPPED)
    positions = lax.broadcasted_iota(jnp.int32, (1, out_grads.shape[1], 1), 1)
    masked = jnp.where(positions < lengths[:, None, None], out_grads, jnp.zeros_like(out_grads))
    masked = jnp.swapaxes(masked, 1, 2)

    step = jnp.array([2 * k for k in ARRIVALS for _ in range(2)], jnp.int32)
    second_core = jnp.array([0, 1] * len(ARRIVALS), jnp.int32)
    order = ((here & ~1) + step + ((here & 1) ^ second_core)) & (devices - 1)

    up1, down1 = along_z(own, 1), along_z(own, -1)
    up2, down2 = along_z(up1, 1), along_z(down1, -1)
    up2, down2, second, masked, order = lax.optimization_barrier((up2, down2, second, masked, order))
    second = lax.all_gather(second, "tensor")
    up3, down3 = along_z(up2, 1), along_z(down2, -1)
    up4, down4 = along_z(up3[:1], 1), along_z(down3[1:], -1)
    pieces = []
    for piece in (own, up1, down1, up2, down2, up3, down3):
        pieces += [piece, crossed(piece, 1)]
    pieces += [up4, crossed(up4, 1), down4, crossed(down4, 1)]

    raw, exponents, squares = raw_products(order, pieces, masked)
    raw = lax.all_to_all(raw, "dp", 0, 0)
    products, top, share = plain_products(second, masked, squares)
    share = share + crossed(share, 1)
    for k in (1, 2, 4):
        share = share + along_z(share, k)
    clipped = clipped_sums(clip_bound, share, products, top, exponents)
    clipped, raw = lax.optimization_barrier((clipped, raw))
    clipped = lax.all_to_all(clipped, "dp", 0, 0)
    return finish(raw, clipped, noise, float((examples * owners) ** -0.5))


def solution(mesh):
    in_specs = (P("dp", "tensor", None), P("dp", None, "tensor"), P("dp"), P(), P("dp", "tensor"))
    out_specs = P("dp", "tensor")
    return jax.shard_map(
        per_device, mesh=mesh, in_specs=in_specs, out_specs=out_specs, check_vma=False
    )
```

```python
import functools

import jax
import jax.numpy as jnp
from jax import lax
from jax.experimental import pallas as pl
from jax.experimental.pallas import tpu as pltpu
from jax.sharding import PartitionSpec as P

LANES = 128
EXTRA = 16
TOGETHER = 8
LEAST = 1e-33
CHUNK = 256
PARAMS = pltpu.CompilerParams(vmem_limit_bytes=56 * 1024 * 1024)
LESS = pltpu.CompilerParams(vmem_limit_bytes=28 * 1024 * 1024)
RAW = ((0, 64), (64, 32))
CLIPPED = ((128, 128), (96, 32))
OWNED = sum(width for _, width in RAW + CLIPPED)
ARRIVALS = (0, -1, 1, -2, 2, -3, 3, 4)
SMALL = pl.CostEstimate(flops=1, bytes_accessed=1, transcendentals=0)


def part_kernel(parts, acts_ref, part_ref):
    at = 0
    for first, width in parts:
        for tile in range(acts_ref.shape[1] // OWNED * width // LANES):
            owners = range(tile * LANES // width, (tile + 1) * LANES // width)
            pieces = [acts_ref[:, o * OWNED + first : o * OWNED + first + width] for o in owners]
            part_ref[:, at : at + LANES] = jnp.concatenate(pieces, axis=1) if len(pieces) > 1 else pieces[0]
            at += LANES


def part_features(acts, parts):
    examples, shard, features = acts.shape
    taken = features // OWNED * sum(width for _, width in parts)
    return pl.pallas_call(
        functools.partial(part_kernel, parts),
        grid=(examples,),
        in_specs=[pl.BlockSpec((shard, features), lambda e: (e, 0))],
        out_specs=pl.BlockSpec((shard, taken), lambda e: (e, 0)),
        out_shape=jax.ShapeDtypeStruct((examples * shard, taken), acts.dtype),
        compiler_params=PARAMS,
    )(acts.reshape(examples * shard, features)).reshape(examples, shard, taken)


def tops(values):
    return jnp.max(jnp.abs(values), axis=0, keepdims=True)


def coded(values, top):
    exponent = jnp.ceil(jnp.log2(jnp.maximum(top, LEAST)) - 14.99)
    return jnp.round(values * jnp.exp2(-exponent)), exponent


def narrow(units):
    return units.astype(jnp.int32).astype(jnp.int16)


def packed(tile, owners):
    if owners == 1:
        return [tile]
    width, rows = LANES // owners, tile.shape[0] // owners
    lane = lax.broadcasted_iota(jnp.int32, (rows, LANES), 1)
    out = []
    for owner in range(owners):
        total = None
        for group in range(owners):
            piece = tile[group * rows : (group + 1) * rows]
            shift = (group - owner) * width % LANES
            piece = pltpu.roll(piece, shift, 1) if shift else piece
            total = piece if total is None else jnp.where(lane >= group * width, piece, total)
        out.append(total)
    return out


def packed_row(row, owners):
    return [t[0:1] for t in packed(jnp.broadcast_to(row, (8 * owners, LANES)), owners)]


def lane_sums(product):
    rows = jnp.sum(product * product, axis=0, keepdims=True)
    return sum(rows[:, at : at + LANES] for at in range(0, rows.shape[1], LANES))


def raw_kernel(order_ref, *refs):
    pieces, (grads_ref, coded_ref, exponent_ref, squares_ref, acts, grads, sems) = refs[:-7], refs[-7:]
    example = pl.program_id(0)
    depth = pieces[0].shape[1]

    def copies(e):
        far = pieces[-4 + 2 * e : len(pieces) - 2 + 2 * e]
        sources = [p.at[e] for p in pieces[:-4]] + [p.at[0] for p in far]
        made = [pltpu.make_async_copy(grads_ref.at[e], grads.at[e], sems.at[e, len(sources)])]
        for k, source in enumerate(sources):
            place = pl.ds(pl.multiple_of(order_ref[k] * depth, depth), depth)
            made.append(pltpu.make_async_copy(source, acts.at[e, place], sems.at[e, k]))
        return made

    @pl.when(example == 0)
    def _():
        for copy in copies(0):
            copy.start()
        for copy in copies(0):
            copy.wait()
        for copy in copies(1):
            copy.start()

    @pl.when(example == 1)
    def _():
        for copy in copies(1):
            copy.wait()

    columns = grads.shape[1]
    squares = jnp.zeros((1, LANES), jnp.float32)
    at = row = 0
    for h, (_, width) in enumerate(RAW):
        together = LANES // width
        rows = columns // together
        for tile in range(coded_ref.shape[0] // together):
            if at % CHUNK == 0:
                some = acts[example, :, at : at + CHUNK]
                product = jnp.dot(grads[example], some, preferred_element_type=jnp.float32)
                squares = squares + lane_sums(product)
            values = product[:, at % CHUNK : at % CHUNK + LANES]
            units, exponent = coded(values, tops(values))
            exponents = packed_row(exponent, together)
            for k, block in enumerate(packed(units, together)):
                coded_ref[tile * together + k, 0, row : row + rows] = narrow(block)
                exponent_ref[tile * together + k, 0, h : h + 1] = exponents[k]
            at += LANES
        row += rows
    squares_ref[0] = squares


def raw_products(order, pieces, grads):
    examples, shard, features = pieces[0].shape
    _, columns, positions = grads.shape
    owners = features // sum(width for _, width in RAW)
    rows = columns * features // owners // LANES
    return pl.pallas_call(
        raw_kernel,
        grid=(examples,),
        in_specs=[pl.BlockSpec(memory_space=pltpu.SMEM)]
        + [pl.BlockSpec(memory_space=pltpu.HBM)] * (len(pieces) + 1),
        out_specs=[
            pl.BlockSpec((owners, 1, rows, LANES), lambda e: (0, e, 0, 0)),
            pl.BlockSpec((owners, 1, 8, LANES), lambda e: (0, e, 0, 0)),
            pl.BlockSpec((1, 1, LANES), lambda e: (e, 0, 0)),
        ],
        out_shape=[
            jax.ShapeDtypeStruct((owners, examples, rows, LANES), jnp.int16),
            jax.ShapeDtypeStruct((owners, examples, 8, LANES), jnp.float32),
            jax.ShapeDtypeStruct((examples, 1, LANES), jnp.float32),
        ],
        scratch_shapes=[
            pltpu.VMEM((examples, positions, features), pieces[0].dtype),
            pltpu.VMEM(grads.shape, grads.dtype),
            pltpu.SemaphoreType.DMA((examples, len(order) + 1)),
        ],
        compiler_params=PARAMS,
    )(order, *pieces, grads)


def plain_kernel(acts_ref, grads_ref, squares_ref, product_ref, top_ref, share_ref, acts, grads, acts_sems, grads_sems):
    devices, examples, shard, _ = acts_ref.shape
    width = product_ref.shape[2]
    tiles = acts_ref.shape[3] // width
    example, tile = pl.program_id(0), pl.program_id(1)

    step = example * tiles + tile
    halves = ((0, 2 * CHUNK), (2 * CHUNK, width - 2 * CHUNK))

    def acts_copies(e, i):
        slot = (e * tiles + i) % 2
        made = []
        for half, (first, wide) in enumerate(halves):
            here = pl.ds(pl.multiple_of(i * width + first, LANES), wide)
            place = acts.at[slot, :, :, pl.ds(first, wide)]
            made.append(pltpu.make_async_copy(acts_ref.at[:, e, :, here], place, acts_sems.at[slot, half]))
        return made

    def grads_copy(e):
        return pltpu.make_async_copy(grads_ref.at[e], grads.at[e], grads_sems.at[e])

    @pl.when(step == 0)
    def _():
        grads_copy(0).start()
        for copy in acts_copies(0, 0):
            copy.start()

    @pl.when(tile == 0)
    def _():
        grads_copy(example).wait()
        share_ref[...] = squares_ref[...]

    now = acts_copies(example, tile)
    slot = step % 2
    share = share_ref[0]
    for at in range(0, width, CHUNK):
        if at == halves[0][0]:
            now[0].wait()
        if at == halves[1][0]:
            now[1].wait()

            @pl.when(step + 1 < examples * tiles)
            def _():
                for copy in acts_copies((step + 1) // tiles, (step + 1) % tiles):
                    copy.start()

            @pl.when(step == 0)
            def _():
                for e in range(1, examples):
                    grads_copy(e).start()

        here = slice(at, at + CHUNK)
        some = acts[slot, :, :, here].reshape(devices * shard, CHUNK)
        product = jnp.dot(grads[example], some, preferred_element_type=jnp.float32)
        product_ref[0, :, here] = product
        top_ref[0, :, here] = tops(product)
        share = share + lane_sums(product)
    share_ref[0] = share


def plain_products(acts, grads, squares):
    devices, examples, shard, features = acts.shape
    _, columns, _ = grads.shape
    width = features // 2
    row = pl.BlockSpec((1, 1, LANES), lambda e, i: (e, 0, 0))
    hbm = pl.BlockSpec(memory_space=pltpu.HBM)
    return pl.pallas_call(
        plain_kernel,
        grid=(examples, features // width),
        in_specs=[hbm, hbm, row],
        out_specs=[
            pl.BlockSpec((1, columns, width), lambda e, i: (e, 0, i)),
            pl.BlockSpec((1, 1, width), lambda e, i: (e, 0, i)),
            row,
        ],
        out_shape=[
            jax.ShapeDtypeStruct((examples, columns, features), jnp.float32),
            jax.ShapeDtypeStruct((examples, 1, features), jnp.float32),
            jax.ShapeDtypeStruct((examples, 1, LANES), jnp.float32),
        ],
        scratch_shapes=[
            pltpu.VMEM((2, devices, shard, width), acts.dtype),
            pltpu.VMEM(grads.shape, grads.dtype),
            pltpu.SemaphoreType.DMA((2, 2)),
            pltpu.SemaphoreType.DMA((examples,)),
        ],
        cost_estimate=SMALL,
        compiler_params=LESS,
    )(*(pltpu.with_memory_space_constraint(a, pltpu.HBM) for a in (acts, grads, squares)))


def clipped_kernel(clip_ref, shares_ref, wide_ref, thin_ref, wide_top_ref, thin_top_ref, exponent_ref, coded_ref):
    examples, columns, _ = wide_ref.shape
    owners = coded_ref.shape[0]
    clip = clip_ref[0]
    blank = jnp.zeros((1, LANES), jnp.float32)
    factors, extra = [], [[] for _ in range(owners)]
    for e in range(examples):
        square = jnp.sum(shares_ref[e], axis=1, keepdims=True)
        factor = clip / jnp.maximum(jnp.sqrt(square), clip)
        factors.append(factor)
        power = jnp.floor(jnp.log2(jnp.maximum(factor, LEAST))) + 1.0
        scaled = factor * jnp.exp2(-power) * 16384.0
        high = jnp.floor(scaled)
        low = jnp.round((scaled - high) * 16384.0)
        for k in range(owners):
            extra[k] += [blank + high, blank + low]
            extra[k] += [exponent_ref[k, e, h : h + 1] + power for h in range(len(RAW))]

    def added(ref, *at):
        return sum(factors[e] * ref[(e,) + at] for e in range(examples))

    everything = slice(None)
    thin_units, exponent = coded(added(thin_ref, everything, everything), added(thin_top_ref, everything, everything))
    thin_units, thin_exponents = packed(thin_units, owners), packed_row(exponent, owners)
    for k in range(owners):
        here = slice(k * LANES, (k + 1) * LANES)
        top = added(wide_top_ref, everything, here)
        for at in range(0, columns, LANES):
            rows = slice(at, at + LANES)
            units, exponent = coded(added(wide_ref, rows, here), top)
            coded_ref[k, rows] = narrow(units)
        rows = extra[k] + [exponent, thin_exponents[k]]
        rows = jnp.concatenate(rows + [blank] * (EXTRA - len(rows)), axis=0)
        coded_ref[k, columns : coded_ref.shape[1] - EXTRA] = narrow(thin_units[k])
        coded_ref[k, coded_ref.shape[1] - EXTRA :] = narrow(rows)


def clipped_sums(clip_bound, shares, products, top, exponents):
    examples, columns, features = products.shape
    owners = exponents.shape[0]
    together = LANES // CLIPPED[1][1]
    rows = columns * features // owners // LANES + EXTRA
    return pl.pallas_call(
        clipped_kernel,
        grid=(owners // together,),
        in_specs=[
            pl.BlockSpec(memory_space=pltpu.SMEM),
            pl.BlockSpec(shares.shape, lambda i: (0, 0, 0)),
            pl.BlockSpec((examples, columns, together * LANES), lambda i: (0, 0, i)),
            pl.BlockSpec((examples, columns, LANES), lambda i: (0, 0, owners + i)),
            pl.BlockSpec((examples, 1, together * LANES), lambda i: (0, 0, i)),
            pl.BlockSpec((examples, 1, LANES), lambda i: (0, 0, owners + i)),
            pl.BlockSpec((together, examples, 8, LANES), lambda i: (i, 0, 0, 0)),
        ],
        out_specs=pl.BlockSpec((together, rows, LANES), lambda i: (i, 0, 0)),
        out_shape=jax.ShapeDtypeStruct((owners, rows, LANES), jnp.int16),
        cost_estimate=SMALL,
        compiler_params=LESS,
    )(clip_bound, shares, products, products, top, top, exponents)


def finish_kernel(scale, raw_ref, clipped_ref, noise_ref, out_ref, raw_sum, clipped_sum):
    _, examples, _, _ = raw_ref.shape
    columns = out_ref.shape[1]
    group = pl.program_id(0)

    @pl.when(group == 0)
    def _():
        raw_sum[...] = jnp.zeros_like(raw_sum)
        clipped_sum[...] = jnp.zeros_like(clipped_sum)

    kinds = len(RAW)
    bottom = clipped_sum.shape[0]
    extra = [clipped_ref[g, bottom:].astype(jnp.float32) for g in range(TOGETHER)]
    row = lambda g, k: extra[g][k : k + 1]
    at = 0
    for h, (_, width) in enumerate(RAW):
        weights = []
        for g in range(TOGETHER):
            for e in range(examples):
                base = e * (2 + kinds)
                weight = (row(g, base) + row(g, base + 1) * (1.0 / 16384.0)) * (1.0 / 16384.0)
                weights.append((g, e, weight * jnp.exp2(row(g, base + 2 + h))))
        end = at + columns * width // LANES
        for block in range(at, end, LANES):
            rows = slice(block, block + LANES)
            raw_sum[rows] += sum(w * raw_ref[g, e, rows].astype(jnp.float32) for g, e, w in weights)
        at = end
    at = 0
    for h, (_, width) in enumerate(CLIPPED):
        steps = [jnp.exp2(row(g, examples * (2 + kinds) + h)) for g in range(TOGETHER)]
        end = at + columns * width // LANES
        for block in range(at, end, LANES):
            rows = slice(block, block + LANES)
            clipped_sum[rows] += sum(w * clipped_ref[g, rows].astype(jnp.float32) for g, w in enumerate(steps))
        at = end

    @pl.when(group == pl.num_programs(0) - 1)
    def _():
        for sums, parts in ((raw_sum, RAW), (clipped_sum, CLIPPED)):
            at = 0
            for first, width in parts:
                together = LANES // width
                rows = columns // together
                turned = sums[at : at + rows].T
                for k in range(together):
                    here = (slice(first, first + width), slice(k * rows, (k + 1) * rows))
                    out_ref[here] = turned[k * width : (k + 1) * width] * scale + noise_ref[here]
                at += rows


def finish(raw, clipped, noise, scale):
    groups, examples, raw_rows, _ = raw.shape
    rows = clipped.shape[1]
    whole = pl.BlockSpec(noise.shape, lambda g: (0, 0))
    return pl.pallas_call(
        functools.partial(finish_kernel, scale),
        grid=(groups // TOGETHER,),
        in_specs=[
            pl.BlockSpec((TOGETHER, examples, raw_rows, LANES), lambda g: (g, 0, 0, 0)),
            pl.BlockSpec((TOGETHER, rows, LANES), lambda g: (g, 0, 0)),
            whole,
        ],
        out_specs=whole,
        out_shape=jax.ShapeDtypeStruct(noise.shape, jnp.float32),
        scratch_shapes=[pltpu.VMEM((raw_rows, LANES), jnp.float32), pltpu.VMEM((rows - EXTRA, LANES), jnp.float32)],
        compiler_params=PARAMS,
    )(raw, clipped, noise)


def per_device(activations, out_grads, lengths, clip_bound, noise):
    owners = lax.axis_size("dp")
    devices = lax.axis_size("tensor")
    examples = activations.shape[0]
    here = lax.axis_index("tensor")

    def along_z(x, k):
        return lax.ppermute(x, "tensor", [(t, (t + 2 * k) % devices) for t in range(devices)])

    def crossed(x, k):
        return lax.ppermute(x, "tensor", [(t, t ^ k) for t in range(devices)])

    own = part_features(activations, RAW)
    second = part_features(activations, CLIPPED)
    positions = lax.broadcasted_iota(jnp.int32, (1, out_grads.shape[1], 1), 1)
    masked = jnp.where(positions < lengths[:, None, None], out_grads, jnp.zeros_like(out_grads))
    masked = jnp.swapaxes(masked, 1, 2)

    step = jnp.array([2 * k for k in ARRIVALS for _ in range(2)], jnp.int32)
    second_core = jnp.array([0, 1] * len(ARRIVALS), jnp.int32)
    order = ((here & ~1) + step + ((here & 1) ^ second_core)) & (devices - 1)

    up1, down1 = along_z(own, 1), along_z(own, -1)
    up2, down2 = along_z(up1, 1), along_z(down1, -1)
    up2, down2, second, masked, order = lax.optimization_barrier((up2, down2, second, masked, order))
    second = lax.all_gather(second, "tensor")
    up3, down3 = along_z(up2, 1), along_z(down2, -1)
    up4, down4 = along_z(up3[:1], 1), along_z(down3[1:], -1)
    pieces = []
    for piece in (own, up1, down1, up2, down2, up3, down3):
        pieces += [piece, crossed(piece, 1)]
    pieces += [up4, crossed(up4, 1), down4, crossed(down4, 1)]

    raw, exponents, squares = raw_products(order, pieces, masked)
    raw = lax.all_to_all(raw, "dp", 0, 0)
    products, top, share = plain_products(second, masked, squares)
    share = share + crossed(share, 1) + crossed(share, 2) + crossed(share, 3)
    share = share + crossed(share, 4) + crossed(share, 8) + crossed(share, 12)
    clipped = clipped_sums(clip_bound, share, products, top, exponents)
    clipped, raw = lax.optimization_barrier((clipped, raw))
    clipped = lax.all_to_all(clipped, "dp", 0, 0)
    return finish(raw, clipped, noise, float((examples * owners) ** -0.5))


def solution(mesh):
    in_specs = (P("dp", "tensor", None), P("dp", None, "tensor"), P("dp"), P(), P("dp", "tensor"))
    out_specs = P("dp", "tensor")
    return jax.shard_map(
        per_device, mesh=mesh, in_specs=in_specs, out_specs=out_specs, check_vma=False
    )
```

```python
import functools

import jax
import jax.numpy as jnp
from jax import lax
from jax.experimental import pallas as pl
from jax.experimental.pallas import tpu as pltpu
from jax.sharding import PartitionSpec as P

LANES = 128
EXTRA = 16
TOGETHER = 8
LEAST = 1e-33
CHUNK = 256
PARAMS = pltpu.CompilerParams(vmem_limit_bytes=56 * 1024 * 1024)
LESS = pltpu.CompilerParams(vmem_limit_bytes=28 * 1024 * 1024)
RAW = ((0, 64), (64, 32))
CLIPPED = ((128, 128), (96, 32))
OWNED = sum(width for _, width in RAW + CLIPPED)
ARRIVALS = (0, -1, 1, -2, 2, -3, 3, 4)
SMALL = pl.CostEstimate(flops=1, bytes_accessed=1, transcendentals=0)


def part_kernel(parts, acts_ref, part_ref):
    at = 0
    for first, width in parts:
        for tile in range(acts_ref.shape[1] // OWNED * width // LANES):
            owners = range(tile * LANES // width, (tile + 1) * LANES // width)
            pieces = [acts_ref[:, o * OWNED + first : o * OWNED + first + width] for o in owners]
            part_ref[:, at : at + LANES] = jnp.concatenate(pieces, axis=1) if len(pieces) > 1 else pieces[0]
            at += LANES


def part_features(acts, parts):
    examples, shard, features = acts.shape
    taken = features // OWNED * sum(width for _, width in parts)
    return pl.pallas_call(
        functools.partial(part_kernel, parts),
        grid=(examples,),
        in_specs=[pl.BlockSpec((shard, features), lambda e: (e, 0))],
        out_specs=pl.BlockSpec((shard, taken), lambda e: (e, 0)),
        out_shape=jax.ShapeDtypeStruct((examples * shard, taken), acts.dtype),
        compiler_params=PARAMS,
    )(acts.reshape(examples * shard, features)).reshape(examples, shard, taken)


def tops(values):
    return jnp.max(jnp.abs(values), axis=0, keepdims=True)


def coded(values, top):
    exponent = jnp.ceil(jnp.log2(jnp.maximum(top, LEAST)) - 14.99)
    return jnp.round(values * jnp.exp2(-exponent)), exponent


def narrow(units):
    return units.astype(jnp.int32).astype(jnp.int16)


def packed(tile, owners):
    if owners == 1:
        return [tile]
    width, rows = LANES // owners, tile.shape[0] // owners
    lane = lax.broadcasted_iota(jnp.int32, (rows, LANES), 1)
    out = []
    for owner in range(owners):
        total = None
        for group in range(owners):
            piece = tile[group * rows : (group + 1) * rows]
            shift = (group - owner) * width % LANES
            piece = pltpu.roll(piece, shift, 1) if shift else piece
            total = piece if total is None else jnp.where(lane >= group * width, piece, total)
        out.append(total)
    return out


def packed_row(row, owners):
    return [t[0:1] for t in packed(jnp.broadcast_to(row, (8 * owners, LANES)), owners)]


def lane_sums(product):
    rows = jnp.sum(product * product, axis=0, keepdims=True)
    return sum(rows[:, at : at + LANES] for at in range(0, rows.shape[1], LANES))


def raw_kernel(order_ref, *refs):
    pieces, (grads_ref, coded_ref, exponent_ref, squares_ref, acts, grads, sems) = refs[:-7], refs[-7:]
    example = pl.program_id(0)
    depth = pieces[0].shape[1]

    def copies(e):
        far = pieces[-4 + 2 * e : len(pieces) - 2 + 2 * e]
        sources = [p.at[e] for p in pieces[:-4]] + [p.at[0] for p in far]
        made = [pltpu.make_async_copy(grads_ref.at[e], grads.at[e], sems.at[e, len(sources)])]
        for k, source in enumerate(sources):
            place = pl.ds(pl.multiple_of(order_ref[k] * depth, depth), depth)
            made.append(pltpu.make_async_copy(source, acts.at[e, place], sems.at[e, k]))
        return made

    @pl.when(example == 0)
    def _():
        for copy in copies(0) + copies(1):
            copy.start()
        for copy in copies(0):
            copy.wait()

    @pl.when(example == 1)
    def _():
        for copy in copies(1):
            copy.wait()

    columns = grads.shape[1]
    squares = jnp.zeros((1, LANES), jnp.float32)
    at = row = 0
    for h, (_, width) in enumerate(RAW):
        together = LANES // width
        rows = columns // together
        for tile in range(coded_ref.shape[0] // together):
            if at % CHUNK == 0:
                some = acts[example, :, at : at + CHUNK]
                product = jnp.dot(grads[example], some, preferred_element_type=jnp.float32)
                squares = squares + lane_sums(product)
            values = product[:, at % CHUNK : at % CHUNK + LANES]
            units, exponent = coded(values, tops(values))
            exponents = packed_row(exponent, together)
            for k, block in enumerate(packed(units, together)):
                coded_ref[tile * together + k, 0, row : row + rows] = narrow(block)
                exponent_ref[tile * together + k, 0, h : h + 1] = exponents[k]
            at += LANES
        row += rows
    squares_ref[0] = squares


def raw_products(order, pieces, grads):
    examples, shard, features = pieces[0].shape
    _, columns, positions = grads.shape
    owners = features // sum(width for _, width in RAW)
    rows = columns * features // owners // LANES
    return pl.pallas_call(
        raw_kernel,
        grid=(examples,),
        in_specs=[pl.BlockSpec(memory_space=pltpu.SMEM)]
        + [pl.BlockSpec(memory_space=pltpu.HBM)] * (len(pieces) + 1),
        out_specs=[
            pl.BlockSpec((owners, 1, rows, LANES), lambda e: (0, e, 0, 0)),
            pl.BlockSpec((owners, 1, 8, LANES), lambda e: (0, e, 0, 0)),
            pl.BlockSpec((1, 1, LANES), lambda e: (e, 0, 0)),
        ],
        out_shape=[
            jax.ShapeDtypeStruct((owners, examples, rows, LANES), jnp.int16),
            jax.ShapeDtypeStruct((owners, examples, 8, LANES), jnp.float32),
            jax.ShapeDtypeStruct((examples, 1, LANES), jnp.float32),
        ],
        scratch_shapes=[
            pltpu.VMEM((examples, positions, features), pieces[0].dtype),
            pltpu.VMEM(grads.shape, grads.dtype),
            pltpu.SemaphoreType.DMA((examples, len(order) + 1)),
        ],
        compiler_params=PARAMS,
    )(order, *pieces, grads)


def plain_kernel(acts_ref, grads_ref, squares_ref, product_ref, top_ref, share_ref, acts, grads, acts_sems, grads_sems):
    devices, examples, shard, _ = acts_ref.shape
    width = product_ref.shape[2]
    tiles = acts_ref.shape[3] // width
    example, tile = pl.program_id(0), pl.program_id(1)

    def acts_copy(step):
        here = pl.ds(step % tiles * width, width)
        source = acts_ref.at[:, step // tiles, :, here]
        return pltpu.make_async_copy(source, acts.at[step % 2], acts_sems.at[step % 2])

    def grads_copy(e):
        return pltpu.make_async_copy(grads_ref.at[e], grads.at[e], grads_sems.at[e])

    for step in range(examples * tiles):

        @pl.when(example * tiles + tile == step)
        def _():
            if step == 0:
                grads_copy(0).start()
                acts_copy(0).start()
            acts_copy(step).wait()
            if step % tiles == 0:
                grads_copy(step // tiles).wait()
            if step + 1 < examples * tiles:
                acts_copy(step + 1).start()
            if step == 0:
                for e in range(1, examples):
                    grads_copy(e).start()

    @pl.when(tile == 0)
    def _():
        share_ref[...] = squares_ref[...]

    slot = (example * tiles + tile) % 2
    share = share_ref[0]
    for at in range(0, width, CHUNK):
        here = slice(at, at + CHUNK)
        some = acts[slot, :, :, here].reshape(devices * shard, CHUNK)
        product = jnp.dot(grads[example], some, preferred_element_type=jnp.float32)
        product_ref[0, :, here] = product
        top_ref[0, :, here] = tops(product)
        share = share + lane_sums(product)
    share_ref[0] = share


def plain_products(acts, grads, squares):
    devices, examples, shard, features = acts.shape
    _, columns, _ = grads.shape
    width = features // 2
    row = pl.BlockSpec((1, 1, LANES), lambda e, i: (e, 0, 0))
    hbm = pl.BlockSpec(memory_space=pltpu.HBM)
    return pl.pallas_call(
        plain_kernel,
        grid=(examples, features // width),
        in_specs=[hbm, hbm, row],
        out_specs=[
            pl.BlockSpec((1, columns, width), lambda e, i: (e, 0, i)),
            pl.BlockSpec((1, 1, width), lambda e, i: (e, 0, i)),
            row,
        ],
        out_shape=[
            jax.ShapeDtypeStruct((examples, columns, features), jnp.float32),
            jax.ShapeDtypeStruct((examples, 1, features), jnp.float32),
            jax.ShapeDtypeStruct((examples, 1, LANES), jnp.float32),
        ],
        scratch_shapes=[
            pltpu.VMEM((2, devices, shard, width), acts.dtype),
            pltpu.VMEM(grads.shape, grads.dtype),
            pltpu.SemaphoreType.DMA((2,)),
            pltpu.SemaphoreType.DMA((examples,)),
        ],
        cost_estimate=SMALL,
        compiler_params=LESS,
    )(*(pltpu.with_memory_space_constraint(a, pltpu.HBM) for a in (acts, grads, squares)))


def clipped_kernel(clip_ref, shares_ref, wide_ref, thin_ref, wide_top_ref, thin_top_ref, exponent_ref, coded_ref):
    examples, columns, _ = wide_ref.shape
    owners = coded_ref.shape[0]
    clip = clip_ref[0]
    blank = jnp.zeros((1, LANES), jnp.float32)
    factors, extra = [], [[] for _ in range(owners)]
    for e in range(examples):
        square = jnp.sum(shares_ref[e], axis=1, keepdims=True)
        factor = clip / jnp.maximum(jnp.sqrt(square), clip)
        factors.append(factor)
        power = jnp.floor(jnp.log2(jnp.maximum(factor, LEAST))) + 1.0
        scaled = factor * jnp.exp2(-power) * 16384.0
        high = jnp.floor(scaled)
        low = jnp.round((scaled - high) * 16384.0)
        for k in range(owners):
            extra[k] += [blank + high, blank + low]
            extra[k] += [exponent_ref[k, e, h : h + 1] + power for h in range(len(RAW))]

    def added(ref, *at):
        return sum(factors[e] * ref[(e,) + at] for e in range(examples))

    everything = slice(None)
    thin_units, exponent = coded(added(thin_ref, everything, everything), added(thin_top_ref, everything, everything))
    thin_units, thin_exponents = packed(thin_units, owners), packed_row(exponent, owners)
    for k in range(owners):
        here = slice(k * LANES, (k + 1) * LANES)
        top = added(wide_top_ref, everything, here)
        for at in range(0, columns, LANES):
            rows = slice(at, at + LANES)
            units, exponent = coded(added(wide_ref, rows, here), top)
            coded_ref[k, rows] = narrow(units)
        rows = extra[k] + [exponent, thin_exponents[k]]
        rows = jnp.concatenate(rows + [blank] * (EXTRA - len(rows)), axis=0)
        coded_ref[k, columns : coded_ref.shape[1] - EXTRA] = narrow(thin_units[k])
        coded_ref[k, coded_ref.shape[1] - EXTRA :] = narrow(rows)


def clipped_sums(clip_bound, shares, products, top, exponents):
    examples, columns, features = products.shape
    owners = exponents.shape[0]
    together = LANES // CLIPPED[1][1]
    rows = columns * features // owners // LANES + EXTRA
    return pl.pallas_call(
        clipped_kernel,
        grid=(owners // together,),
        in_specs=[
            pl.BlockSpec(memory_space=pltpu.SMEM),
            pl.BlockSpec(shares.shape, lambda i: (0, 0, 0)),
            pl.BlockSpec((examples, columns, together * LANES), lambda i: (0, 0, i)),
            pl.BlockSpec((examples, columns, LANES), lambda i: (0, 0, owners + i)),
            pl.BlockSpec((examples, 1, together * LANES), lambda i: (0, 0, i)),
            pl.BlockSpec((examples, 1, LANES), lambda i: (0, 0, owners + i)),
            pl.BlockSpec((together, examples, 8, LANES), lambda i: (i, 0, 0, 0)),
        ],
        out_specs=pl.BlockSpec((together, rows, LANES), lambda i: (i, 0, 0)),
        out_shape=jax.ShapeDtypeStruct((owners, rows, LANES), jnp.int16),
        cost_estimate=SMALL,
        compiler_params=LESS,
    )(clip_bound, shares, products, products, top, top, exponents)


def finish_kernel(scale, raw_ref, clipped_ref, noise_ref, out_ref, raw_sum, clipped_sum):
    _, examples, _, _ = raw_ref.shape
    columns = out_ref.shape[1]
    group = pl.program_id(0)

    @pl.when(group == 0)
    def _():
        raw_sum[...] = jnp.zeros_like(raw_sum)
        clipped_sum[...] = jnp.zeros_like(clipped_sum)

    kinds = len(RAW)
    bottom = clipped_sum.shape[0]
    extra = [clipped_ref[g, bottom:].astype(jnp.float32) for g in range(TOGETHER)]
    row = lambda g, k: extra[g][k : k + 1]
    at = 0
    for h, (_, width) in enumerate(RAW):
        weights = []
        for g in range(TOGETHER):
            for e in range(examples):
                base = e * (2 + kinds)
                weight = (row(g, base) + row(g, base + 1) * (1.0 / 16384.0)) * (1.0 / 16384.0)
                weights.append((g, e, weight * jnp.exp2(row(g, base + 2 + h))))
        end = at + columns * width // LANES
        for block in range(at, end, LANES):
            rows = slice(block, block + LANES)
            raw_sum[rows] += sum(w * raw_ref[g, e, rows].astype(jnp.float32) for g, e, w in weights)
        at = end
    at = 0
    for h, (_, width) in enumerate(CLIPPED):
        steps = [jnp.exp2(row(g, examples * (2 + kinds) + h)) for g in range(TOGETHER)]
        end = at + columns * width // LANES
        for block in range(at, end, LANES):
            rows = slice(block, block + LANES)
            clipped_sum[rows] += sum(w * clipped_ref[g, rows].astype(jnp.float32) for g, w in enumerate(steps))
        at = end

    @pl.when(group == pl.num_programs(0) - 1)
    def _():
        for sums, parts in ((raw_sum, RAW), (clipped_sum, CLIPPED)):
            at = 0
            for first, width in parts:
                together = LANES // width
                rows = columns // together
                turned = sums[at : at + rows].T
                for k in range(together):
                    here = (slice(first, first + width), slice(k * rows, (k + 1) * rows))
                    out_ref[here] = turned[k * width : (k + 1) * width] * scale + noise_ref[here]
                at += rows


def finish(raw, clipped, noise, scale):
    groups, examples, raw_rows, _ = raw.shape
    rows = clipped.shape[1]
    whole = pl.BlockSpec(noise.shape, lambda g: (0, 0))
    return pl.pallas_call(
        functools.partial(finish_kernel, scale),
        grid=(groups // TOGETHER,),
        in_specs=[
            pl.BlockSpec((TOGETHER, examples, raw_rows, LANES), lambda g: (g, 0, 0, 0)),
            pl.BlockSpec((TOGETHER, rows, LANES), lambda g: (g, 0, 0)),
            whole,
        ],
        out_specs=whole,
        out_shape=jax.ShapeDtypeStruct(noise.shape, jnp.float32),
        scratch_shapes=[pltpu.VMEM((raw_rows, LANES), jnp.float32), pltpu.VMEM((rows - EXTRA, LANES), jnp.float32)],
        compiler_params=PARAMS,
    )(raw, clipped, noise)


def per_device(activations, out_grads, lengths, clip_bound, noise):
    owners = lax.axis_size("dp")
    devices = lax.axis_size("tensor")
    examples = activations.shape[0]
    here = lax.axis_index("tensor")

    def along_z(x, k):
        return lax.ppermute(x, "tensor", [(t, (t + 2 * k) % devices) for t in range(devices)])

    def crossed(x, k):
        return lax.ppermute(x, "tensor", [(t, t ^ k) for t in range(devices)])

    own = part_features(activations, RAW)
    second = part_features(activations, CLIPPED)
    positions = lax.broadcasted_iota(jnp.int32, (1, out_grads.shape[1], 1), 1)
    masked = jnp.where(positions < lengths[:, None, None], out_grads, jnp.zeros_like(out_grads))
    masked = jnp.swapaxes(masked, 1, 2)

    step = jnp.array([2 * k for k in ARRIVALS for _ in range(2)], jnp.int32)
    second_core = jnp.array([0, 1] * len(ARRIVALS), jnp.int32)
    order = ((here & ~1) + step + ((here & 1) ^ second_core)) & (devices - 1)

    up1, down1 = along_z(own, 1), along_z(own, -1)
    up2, down2 = along_z(up1, 1), along_z(down1, -1)
    up2, down2, second, masked, order = lax.optimization_barrier((up2, down2, second, masked, order))
    second = lax.all_gather(second, "tensor")
    up3, down3 = along_z(up2, 1), along_z(down2, -1)
    up4, down4 = along_z(up3[:1], 1), along_z(down3[1:], -1)
    pieces = []
    for piece in (own, up1, down1, up2, down2, up3, down3):
        pieces += [piece, crossed(piece, 1)]
    pieces += [up4, crossed(up4, 1), down4, crossed(down4, 1)]

    raw, exponents, squares = raw_products(order, pieces, masked)
    raw = lax.all_to_all(raw, "dp", 0, 0)
    products, top, share = plain_products(second, masked, squares)
    share = share + crossed(share, 1) + crossed(share, 2) + crossed(share, 3)
    share = share + crossed(share, 4) + crossed(share, 8) + crossed(share, 12)
    clipped = clipped_sums(clip_bound, share, products, top, exponents)
    clipped, raw = lax.optimization_barrier((clipped, raw))
    clipped = lax.all_to_all(clipped, "dp", 0, 0)
    return finish(raw, clipped, noise, float((examples * owners) ** -0.5))


def solution(mesh):
    in_specs = (P("dp", "tensor", None), P("dp", None, "tensor"), P("dp"), P(), P("dp", "tensor"))
    out_specs = P("dp", "tensor")
    return jax.shard_map(
        per_device, mesh=mesh, in_specs=in_specs, out_specs=out_specs, check_vma=False
    )
```
